32 devices in a mesh: blk: 8 (over y, x, core), rows: 4 (over z).
Axes of the slice: x: 2, y: 2, z: 4, core: 2. Of those that a mesh axis runs over, the one named last changes fastest.
Arguments:
- excitations: float32 [64, 16384], P(None, ('blk', 'rows')), may hold values from -6 to 6
- adjoint_loads: float32 [64, 16384], P(None, ('blk', 'rows')), may hold values from -6 to 6
- near_tiles: bfloat16 [1024, 256, 256], P(('blk', 'rows')), may hold values from -0.125 to 0.125
- tile_rows: int32 [1024], P(('blk', 'rows')), may hold values from 0 to 1
- tile_cols: int32 [1024], P(('blk', 'rows')), may hold values from 0 to 7
- tile_count: int32 [32], P(('blk', 'rows')), may hold values from 4 to 32, as said below
- skeleton_in: bfloat16 [1024, 16384], P(None, ('blk', 'rows')), may hold values from -0.125 to 0.125
- skeleton_out: bfloat16 [1024, 16384], P(None, ('blk', 'rows')), may hold values from -0.1875 to 0.1875
- translation: float32 [8, 7, 1024, 1024], P('blk', None, 'rows'), may hold values from -0.0625 to 0.0625
Outputs:
- response: float32 [64, 16384], P(None, ('blk', 'rows'))
- sensitivity: float32 [64, 16384], P(None, ('blk', 'rows'))
The draws below stay inside these ranges and needn't reach their ends.
Inputs may be any that keep to these rules, and one draw needn't show every extreme that they name: `tile_count`: slots of a device are used from slot 0 on; later slots are no part of the operator.
All inputs are finite; a program needn't handle non-finite values.
Results may differ from the reference program's by a relative error of at most 0.0036.
Values may be sent and summed in bfloat16 or wider, within the bound.
A program may use at most 128 MiB of HBM per device.

```python
import jax
import jax.numpy as jnp
from jax import lax

E = 64
S = 1024
TB = 256
TPB = 16
P_DEV = 512
CLUSTER = 2048
CLUSTERS = 8
PANELS = 16384
RB = 2
CBLK = 8
CAP = 32
N_BLK = 8
N_ROWS = 4
DEVICES = 32


def draw_tile_count(key, part):
    first_draw = jax.random.randint(jax.random.fold_in(key, 11), (DEVICES,), CAP // 8, CAP + 1)
    second_draw = jax.random.randint(jax.random.fold_in(key, 12), (DEVICES,), CAP // 8, CAP + 1)
    counts = jnp.minimum(first_draw, second_draw)
    busiest = jax.random.randint(jax.random.fold_in(key, 13), (), 0, DEVICES)
    return counts.at[busiest].set(CAP).astype(jnp.int32)


def plant(entries, key, least, top_value):
    extent = entries.shape
    place = [jax.random.randint(jax.random.fold_in(key, axis), (), 0, extent[axis]) for axis in range(len(extent))]
    entries = entries.at[tuple(place)].set(least)
    longest = extent.index(max(extent))
    place[longest] = (place[longest] + 1) % extent[longest]
    return entries.at[tuple(place)].set(top_value)


def shard_levels(key, shape, split, smallest, high):
    factor_of, own = 1.0, jax.random.fold_in(key, 6)
    for position, parts in split:
        heights = jnp.exp(jax.random.uniform(jax.random.fold_in(own, position), (parts,), jnp.float32, smallest / len(split), high / len(split)))
        factor_of = factor_of * jnp.repeat(heights, shape[position] // parts).reshape([-1 if axis == position else 1 for axis in range(len(shape))])
    return factor_of


def normal_values(stream_key, dims, deviation, bound, pieces=(), kind=jnp.bfloat16):
    level = shard_levels(stream_key, dims, pieces, -0.22, 0.18) if pieces else 1.0
    entries = jax.random.normal(stream_key, dims, jnp.float32) * deviation * level
    return jnp.minimum(jnp.maximum(entries, -bound), bound).astype(kind)


def setup_inputs(seed: int = 0) -> dict:
    key_of = jax.random.split(jax.random.key(seed), 10)
    return {
        "excitations": normal_values(key_of[0], (E, PANELS), 1.0, 6.0, ((1, 32),), jnp.float32),
        "adjoint_loads": normal_values(key_of[1], (E, PANELS), 1.0, 6.0, ((1, 32),), jnp.float32),
        "near_tiles": normal_values(key_of[2], (N_BLK * N_ROWS * CAP, TB, TB), (TB * TPB // 2) ** -0.5, 0.125, ((0, 32),)),
        "tile_rows": plant(jax.random.randint(key_of[3], (N_BLK * N_ROWS * CAP,), 0, RB), jax.random.fold_in(key_of[3], 1), 0, RB - 1).astype(jnp.int32),
        "tile_cols": plant(jax.random.randint(key_of[4], (N_BLK * N_ROWS * CAP,), 0, CBLK), jax.random.fold_in(key_of[4], 1), 0, CBLK - 1).astype(jnp.int32),
        "tile_count": draw_tile_count(jax.random.fold_in(key_of[9], 71), 0),
        "skeleton_in": normal_values(key_of[6], (S, PANELS), CLUSTER ** -0.5, 0.125, ((1, 32),)),
        "skeleton_out": normal_values(key_of[7], (S, PANELS), S ** -0.5, 0.1875, ((1, 32),)),
        "translation": normal_values(key_of[8], (N_BLK, N_BLK - 1, S, S), (S * (N_BLK - 1)) ** -0.5, 0.0625, ((0, 8), (2, 4)), jnp.float32),
    }


highest = lax.Precision.HIGHEST


def reference(excitations, adjoint_loads, near_tiles, tile_rows, tile_cols, tile_count, skeleton_in, skeleton_out, translation):
    drive_low = excitations.astype(jnp.bfloat16)
    loads_low = adjoint_loads.astype(jnp.bfloat16)
    per_cluster = CLUSTER // P_DEV

    def near_slot(slot_raw, carry):
        ahead, behind = carry
        slot = jnp.asarray(slot_raw).astype(jnp.int32)
        device = slot // CAP
        live_mask = (slot % CAP < tile_count[device]).astype(jnp.float32)
        row_start = (device * P_DEV + tile_rows[slot] * TB).astype(jnp.int32)
        col_start = ((device // per_cluster) * CLUSTER + tile_cols[slot] * TB).astype(jnp.int32)
        tile_block = near_tiles[slot]
        source = lax.dynamic_slice_in_dim(drive_low, col_start, TB, 1)
        target = lax.dynamic_slice_in_dim(loads_low, row_start, TB, 1)
        forward = lax.dot_general(source, tile_block, (((1,), (1,)), ((), ())), preferred_element_type=jnp.float32) * live_mask
        backward = jnp.dot(target, tile_block, preferred_element_type=jnp.float32) * live_mask
        ahead = lax.dynamic_update_slice_in_dim(ahead, lax.dynamic_slice_in_dim(ahead, row_start, TB, 1) + forward, row_start, 1)
        behind = lax.dynamic_update_slice_in_dim(behind, lax.dynamic_slice_in_dim(behind, col_start, TB, 1) + backward, col_start, 1)
        return ahead, behind

    blank = jnp.zeros((E, PANELS), jnp.float32)
    near_ahead, near_behind = lax.fori_loop(0, N_BLK * N_ROWS * CAP, near_slot, (blank, blank))

    cluster_ids = jnp.arange(CLUSTERS, dtype=jnp.int32)
    lag = jnp.arange(1, CLUSTERS, dtype=jnp.int32)

    def cluster_part(values, matrix, index):
        start = (index * CLUSTER).astype(jnp.int32)
        left = lax.dynamic_slice_in_dim(values, start, CLUSTER, 1)
        right = lax.dynamic_slice_in_dim(matrix, start, CLUSTER, 1)
        return lax.dot_general(left, right, (((1,), (1,)), ((), ())), preferred_element_type=jnp.float32)

    charges = lax.map(lambda index: cluster_part(drive_low, skeleton_in, index), cluster_ids)
    gradient = lax.map(lambda index: cluster_part(loads_low, skeleton_out, index), cluster_ids)

    def forward_far(index):
        sources = jnp.remainder(index - lag, CLUSTERS).astype(jnp.int32)
        potential = jnp.einsum("dej,dkj->ek", charges[sources], translation[index], precision=highest)
        potential_low = potential.astype(jnp.bfloat16)
        start = (index * CLUSTER).astype(jnp.int32)
        return jnp.dot(potential_low, lax.dynamic_slice_in_dim(skeleton_out, start, CLUSTER, 1), preferred_element_type=jnp.float32)

    def backward_far(index):
        senders = jnp.remainder(index + lag, CLUSTERS).astype(jnp.int32)
        potential = jnp.einsum("dek,dkj->ej", gradient[senders], translation[senders, lag - 1], precision=highest)
        adjoint_low = potential.astype(jnp.bfloat16)
        start = (index * CLUSTER).astype(jnp.int32)
        return jnp.dot(adjoint_low, lax.dynamic_slice_in_dim(skeleton_in, start, CLUSTER, 1), preferred_element_type=jnp.float32)

    far_ahead = jnp.transpose(lax.map(forward_far, cluster_ids), (1, 0, 2)).reshape(E, PANELS)
    far_behind = jnp.transpose(lax.map(backward_far, cluster_ids), (1, 0, 2)).reshape(E, PANELS)
    return near_ahead + far_ahead, near_behind + far_behind
```

```python
import functools

import jax
import jax.numpy as jnp
from jax import lax
from jax.experimental import pallas as pl
from jax.experimental.pallas import tpu as pltpu
from jax.sharding import PartitionSpec as P

highest = lax.Precision.HIGHEST


def plain_plan(
    excitations,
    adjoint_loads,
    near_tiles,
    tile_rows,
    tile_cols,
    tile_count,
    skeleton_in,
    skeleton_out,
    translation,
):
    drive_low = excitations.astype(jnp.bfloat16)
    loads_low = adjoint_loads.astype(jnp.bfloat16)
    excite_count = excitations.shape[0]
    panels = excitations.shape[1]
    tile_size = near_tiles.shape[1]
    kernels = translation[0]
    share_width = kernels.shape[1]
    clusters = lax.axis_size("blk")
    cluster = lax.axis_index("blk")
    gathered = lax.all_gather(drive_low, "rows", axis=1, tiled=True)
    column_blocks = gathered.shape[1] // tile_size
    row_blocks = panels // tile_size
    drive_blocks = gathered.reshape(excite_count, column_blocks, tile_size)
    load_blocks = loads_low.reshape(excite_count, row_blocks, tile_size)
    used_slots = tile_count[0]

    def near_group(group_index, carry):
        ahead, behind = carry
        first_slot = group_index * 4
        tile_group = lax.dynamic_slice_in_dim(near_tiles, first_slot, 4, 0)
        row_ids = lax.dynamic_slice_in_dim(tile_rows, first_slot, 4, 0)
        column_ids = lax.dynamic_slice_in_dim(tile_cols, first_slot, 4, 0)
        live_mask = (first_slot + jnp.arange(4, dtype=jnp.int32) < used_slots).astype(jnp.float32)[
            None, :, None
        ]
        source = jnp.take(drive_blocks, column_ids, axis=1)
        target = jnp.take(load_blocks, row_ids, axis=1)
        forward = (
            jnp.einsum("egj,gij->egi", source, tile_group, preferred_element_type=jnp.float32)
            * live_mask
        )
        backward = (
            jnp.einsum("egi,gij->egj", target, tile_group, preferred_element_type=jnp.float32)
            * live_mask
        )
        return (ahead.at[:, row_ids].add(forward), behind.at[:, column_ids].add(backward))

    near_start = (
        jnp.zeros((excite_count, row_blocks, tile_size), jnp.float32),
        jnp.zeros((excite_count, column_blocks, tile_size), jnp.float32),
    )
    near_ahead, near_behind = lax.fori_loop(0, (used_slots + 3) // 4, near_group, near_start)
    contract_panels = (((1,), (1,)), ((), ()))
    charge_part = lax.dot_general(
        drive_low, skeleton_in, contract_panels, preferred_element_type=jnp.float32
    )
    gradient_part = lax.dot_general(
        loads_low, skeleton_out, contract_panels, preferred_element_type=jnp.float32
    )
    charges, gradient_all = lax.psum((charge_part, gradient_part), "rows")
    gradient = lax.dynamic_slice_in_dim(
        gradient_all, lax.axis_index("rows") * share_width, share_width, 1
    )

    def offsets_for(other_ids):
        offset = jnp.remainder(cluster - other_ids, clusters)
        active = (offset != 0).astype(jnp.float32)
        return (jnp.maximum(offset - 1, 0), active)

    charge_piece = lax.all_gather(charges[None], "blk", axis=0, tiled=True)
    span_count = charge_piece.shape[0]
    offset, active = offsets_for(jnp.arange(span_count, dtype=jnp.int32))
    chosen = jnp.take(kernels, offset, axis=0)
    potential = jnp.einsum(
        "cej,ckj->ek", charge_piece * active[:, None, None], chosen, precision=highest
    )
    potential_low = lax.all_gather(potential.astype(jnp.bfloat16), "rows", axis=1, tiled=True)
    far_ahead = jnp.dot(potential_low, skeleton_out, preferred_element_type=jnp.float32)
    offset, active = offsets_for(jnp.arange(lax.axis_size("blk") * 1, dtype=jnp.int32))
    chosen = jnp.take(kernels, offset, axis=0)
    summed = lax.psum_scatter(
        jnp.einsum("ek,ckj->cej", gradient, chosen, precision=highest) * active[:, None, None],
        "blk",
        scatter_dimension=0,
        tiled=True,
    )
    adjoint_low = lax.psum(summed[0], "rows").astype(jnp.bfloat16)
    far_behind = jnp.dot(adjoint_low, skeleton_in, preferred_element_type=jnp.float32)
    near_columns = lax.psum_scatter(
        near_behind.reshape(excite_count, column_blocks * tile_size),
        "rows",
        scatter_dimension=1,
        tiled=True,
    )
    response = near_ahead.reshape(excite_count, panels) + far_ahead
    sensitivity = near_columns + far_behind
    return (response, sensitivity)


MESH = pl.DeviceIdType.MESH
GROUP = 4
bf16 = jnp.bfloat16
f32 = jnp.float32


def dot_nt(a, b):
    return lax.dot_general(a, b, (((1,), (1,)), ((), ())), preferred_element_type=f32)


def dot_nn(a, b):
    return jnp.dot(a, b, preferred_element_type=f32)


def kernel(
    rows,
    clusters,
    count_ref,
    tile_row_ref,
    tile_col_ref,
    drive_ref,
    loads_ref,
    tiles_hbm,
    skin_hbm,
    skout_hbm,
    trans_hbm,
    response_ref,
    sensitivity_ref,
    tiles,
    skin,
    skout,
    trans,
    trans_low,
    drive_all,
    loads_low,
    grad_part,
    grad_send,
    grad_recv,
    charge_part,
    charge_send,
    charge_recv,
    q_all,
    sib_send,
    sib_recv,
    plane_send,
    plane_recv,
    adj_part,
    adj_send,
    adj_recv,
    adj_all,
    pot_all,
    near_fwd,
    near_adj,
    near_send,
    near_recv,
    local_sem,
    send_sem,
    grad_sem,
    charge_sem,
    drive_sem,
    qz_sem,
    qp_sem,
    qs_sem,
    sib_sem,
    plane_sem,
    adj_sem,
    adjall_sem,
    pot_sem,
    near_sem,
):
    chips = clusters // 2
    b = lax.axis_index("blk")
    r = lax.axis_index("rows")
    core = lax.rem(b, 2)
    chip = lax.div(b, 2)
    cap, size = tiles.shape[0], tiles.shape[1]
    share = q_all.shape[3]
    row_blocks = loads_low.shape[0]
    column_blocks = rows * row_blocks
    offsets = trans.shape[0]

    def row_at(step):
        return lax.rem(r + step + rows, rows)

    def blk_at(step, which):
        return lax.rem(chip + step + chips, chips) * 2 + which

    sibling = b + 1 - 2 * core

    local = []

    def fetch(src, dst):
        copy = pltpu.make_async_copy(src, dst, local_sem.at[len(local)])
        copy.start()
        local.append(copy)
        return copy

    get_out = fetch(skout_hbm, skout)
    get_in = fetch(skin_hbm, skin)
    get_trans = [fetch(trans_hbm.at[d], trans.at[d]) for d in range(offsets)]
    get_tiles = fetch(tiles_hbm, tiles)

    sent = []

    def send(src, dst, recv, blk, row):
        copy = pltpu.make_async_remote_copy(
            src_ref=src,
            dst_ref=dst,
            send_sem=send_sem.at[len(sent)],
            recv_sem=recv,
            device_id=(blk, row),
            device_id_type=MESH,
        )
        copy.start()
        sent.append(copy)
        return copy

    barrier = pltpu.get_barrier_semaphore()
    partners = [(b, row_at(o)) for o in range(1, rows)]
    partners += [(blk_at(o, core), r) for o in range(1, chips)]
    partners += [(sibling, r)]
    for partner in partners:
        pl.semaphore_signal(barrier, inc=1, device_id=partner, device_id_type=MESH)

    for i in range(row_blocks):
        loads_low[i] = loads_ref[:, i * size : (i + 1) * size].astype(bf16)
        drive_all[r * row_blocks + i] = drive_ref[:, i * size : (i + 1) * size].astype(bf16)
    loads_wide = loads_ref[...].astype(bf16)
    get_out.wait()
    for j in range(rows):
        part = dot_nt(loads_wide, skout[j * share : (j + 1) * share, :])
        grad_part[j] = part
        grad_send[j] = part.astype(bf16)
    pl.semaphore_wait(barrier, len(partners))
    grad_copies = [
        send(grad_send.at[row_at(o)], grad_recv.at[o - 1], grad_sem.at[o - 1], b, row_at(o))
        for o in range(1, rows)
    ]
    drive_wide = drive_ref[...].astype(bf16)
    get_in.wait()
    for j in range(rows):
        part = dot_nt(drive_wide, skin[j * share : (j + 1) * share, :])
        charge_part[j] = part
        charge_send[j] = part.astype(bf16)
    charge_copies = [
        send(charge_send.at[row_at(o)], charge_recv.at[o - 1], charge_sem.at[o - 1], b, row_at(o))
        for o in range(1, rows)
    ]
    mine = pl.ds(r * row_blocks, row_blocks)
    drive_copies = [
        send(drive_all.at[mine], drive_all.at[mine], drive_sem.at[o - 1], b, row_at(o))
        for o in range(1, rows)
    ]

    for d in range(offsets):
        get_trans[d].wait()
        trans_low[d] = trans[d].astype(bf16)

    for copy in grad_copies:
        copy.wait_recv()
    gradient = grad_part[r]
    for o in range(rows - 1):
        gradient += grad_recv[o].astype(f32)
    grad_high = gradient.astype(bf16)
    grad_rest = (gradient - grad_high.astype(f32)).astype(bf16)
    grad_both = jnp.concatenate([grad_high, grad_rest], axis=0)
    excite = gradient.shape[0]

    for copy in charge_copies:
        copy.wait_recv()
    charge = charge_part[r]
    for o in range(rows - 1):
        charge += charge_recv[o].astype(f32)
    q_all[r, b] = charge.astype(bf16)

    def send_quarter_to_plane(z):
        piece = q_all.at[row_at(-z), b]
        copies = [
            send(piece, piece, qp_sem.at[z, o - 1], blk_at(o, core), r) for o in range(1, chips)
        ]
        return copies, [send(piece, piece, qs_sem.at[z, 0], sibling, r)]

    piece = q_all.at[r, b]
    qz_copies = [send(piece, piece, qz_sem.at[o - 1], b, row_at(o)) for o in range(1, rows)]
    plane_q, sibling_q = [None] * rows, [None] * rows
    plane_q[0], sibling_q[0] = send_quarter_to_plane(0)

    def adjoint_term(target, j):
        index = lax.rem(b - target + clusters, clusters) - 1
        both = dot_nn(grad_both, trans_low[index, :, j * share : (j + 1) * share])
        return both[:excite] + both[excite:]

    sib_copies = []
    for o in range(chips):
        for j in range(rows):
            sib_send[o, j] = adjoint_term(blk_at(o, 1 - core), j).astype(bf16)
        sib_copies.append(send(sib_send.at[o], sib_recv.at[o], sib_sem.at[o], sibling, r))
    for z in range(1, rows):
        qz_copies[z - 1].wait_recv()
        plane_q[z], sibling_q[z] = send_quarter_to_plane(z)
    plane_copies = []
    for o in range(1, chips):
        terms = [adjoint_term(blk_at(o, core), j) for j in range(rows)]
        sib_copies[o].wait_recv()
        for j in range(rows):
            plane_send[o - 1, j] = (terms[j] + sib_recv[o, j].astype(f32)).astype(bf16)
        plane_copies.append(
            send(
                plane_send.at[o - 1],
                plane_recv.at[o - 1],
                plane_sem.at[o - 1],
                blk_at(o, core),
                r,
            )
        )

    used = count_ref[0]
    near_adj[...] = jnp.zeros_like(near_adj)
    near_fwd[...] = jnp.zeros_like(near_fwd)
    get_tiles.wait()

    def adjoint_group(group, carry):
        products, columns = [], []
        for t in range(GROUP):
            slot = group * GROUP + t
            source = loads_low[tile_row_ref[slot]]
            products.append(dot_nn(source, tiles[slot]))
            columns.append(jnp.where(slot < used, tile_col_ref[slot], -1))
        for c in range(column_blocks):
            total = near_adj[c]
            for t in range(GROUP):
                total += products[t] * jnp.where(columns[t] == c, 1.0, 0.0).astype(f32)
            near_adj[c] = total
        return carry

    def forward_group(group, carry):
        products, targets = [], []
        for t in range(GROUP):
            slot = group * GROUP + t
            source = drive_all[tile_col_ref[slot]]
            products.append(dot_nt(source, tiles[slot]))
            targets.append(jnp.where(slot < used, tile_row_ref[slot], -1))
        for i in range(row_blocks):
            total = near_fwd[i]
            for t in range(GROUP):
                total += products[t] * jnp.where(targets[t] == i, 1.0, 0.0).astype(f32)
            near_fwd[i] = total
        return carry

    groups = cap // GROUP
    lax.fori_loop(0, groups, adjoint_group, 0)
    for c in range(column_blocks):
        near_send[c] = near_adj[c].astype(bf16)
    near_copies = [
        send(
            near_send.at[pl.ds(row_at(o) * row_blocks, row_blocks)],
            near_recv.at[o - 1],
            near_sem.at[o - 1],
            b,
            row_at(o),
        )
        for o in range(1, rows)
    ]

    for z in range(rows):
        for o in range(1, chips):
            plane_q[z][o - 1].wait_recv()
            piece = q_all.at[row_at(-z), blk_at(-o, core)]
            sibling_q[z].append(send(piece, piece, qs_sem.at[z, o], sibling, r))

    for copy in drive_copies:
        copy.wait_recv()
    lax.fori_loop(0, groups // 2, forward_group, 0)

    sib_copies[0].wait_recv()
    for copy in plane_copies:
        copy.wait_recv()
    for j in range(rows):
        total = sib_recv[0, j].astype(f32)
        for o in range(chips - 1):
            total += plane_recv[o, j].astype(f32)
        adj_part[j] = total
        adj_send[j] = total.astype(bf16)
    adj_copies = [
        send(adj_send.at[row_at(o)], adj_recv.at[o - 1], adj_sem.at[o - 1], b, row_at(o))
        for o in range(1, rows)
    ]

    lax.fori_loop(groups // 2, groups, forward_group, 0)

    for z in range(rows):
        for copy in sibling_q[z]:
            copy.wait_recv()
    potential = jnp.zeros((excite, share), f32)
    for j in range(rows):
        for d in range(1, offsets + 1):
            source = q_all[j, lax.rem(b - d + clusters, clusters)]
            potential += dot_nt(source, trans_low[d - 1, :, j * share : (j + 1) * share])
    pot_all[r] = potential.astype(bf16)
    piece = pot_all.at[r]
    pot_copies = [send(piece, piece, pot_sem.at[o - 1], b, row_at(o)) for o in range(1, rows)]

    for copy in adj_copies:
        copy.wait_recv()
    adjoint = adj_part[r]
    for o in range(rows - 1):
        adjoint += adj_recv[o].astype(f32)
    adj_all[r] = adjoint.astype(bf16)
    piece = adj_all.at[r]
    adjall_copies = [send(piece, piece, adjall_sem.at[o - 1], b, row_at(o)) for o in range(1, rows)]

    for copy in near_copies:
        copy.wait_recv()
    for i in range(row_blocks):
        total = near_adj[r * row_blocks + i]
        for o in range(rows - 1):
            total += near_recv[o, i].astype(f32)
        near_adj[r * row_blocks + i] = total

    for copy in pot_copies:
        copy.wait_recv()
    for i in range(row_blocks):
        total = near_fwd[i]
        for j in range(rows):
            block = skout[j * share : (j + 1) * share, i * size : (i + 1) * size]
            total += dot_nn(pot_all[j], block)
        response_ref[:, i * size : (i + 1) * size] = total
    for copy in adjall_copies:
        copy.wait_recv()
    for i in range(row_blocks):
        total = near_adj[r * row_blocks + i]
        for j in range(rows):
            block = skin[j * share : (j + 1) * share, i * size : (i + 1) * size]
            total += dot_nn(adj_all[j], block)
        sensitivity_ref[:, i * size : (i + 1) * size] = total
    for copy in sent:
        copy.wait_send()


def fused_plan(
    rows,
    clusters,
    excitations,
    adjoint_loads,
    near_tiles,
    tile_rows,
    tile_cols,
    tile_count,
    skeleton_in,
    skeleton_out,
    translation,
):
    kernels = translation[0]
    excite, panels = excitations.shape
    cap, size = near_tiles.shape[:2]
    offsets, share, points = kernels.shape
    chips = clusters // 2
    row_blocks = panels // size
    blocks = rows * row_blocks
    others = rows - 1
    sends = 7 * others + rows * (chips - 1) + rows * chips + chips + chips - 1 + others
    vmem, dma = pltpu.VMEM, pltpu.SemaphoreType.DMA
    scratch = [
        vmem((cap, size, size), bf16),
        vmem((points, panels), bf16),
        vmem((points, panels), bf16),
        vmem((offsets, share, points), f32),
        vmem((offsets, share, points), bf16),
        vmem((blocks, excite, size), bf16),
        vmem((row_blocks, excite, size), bf16),
        vmem((rows, excite, share), f32),
        vmem((rows, excite, share), bf16),
        vmem((others, excite, share), bf16),
        vmem((rows, excite, share), f32),
        vmem((rows, excite, share), bf16),
        vmem((others, excite, share), bf16),
        vmem((rows, clusters, excite, share), bf16),
        vmem((chips, rows, excite, share), bf16),
        vmem((chips, rows, excite, share), bf16),
        vmem((chips - 1, rows, excite, share), bf16),
        vmem((chips - 1, rows, excite, share), bf16),
        vmem((rows, excite, share), f32),
        vmem((rows, excite, share), bf16),
        vmem((others, excite, share), bf16),
        vmem((rows, excite, share), bf16),
        vmem((rows, excite, share), bf16),
        vmem((row_blocks, excite, size), f32),
        vmem((blocks, excite, size), f32),
        vmem((blocks, excite, size), bf16),
        vmem((others, row_blocks, excite, size), bf16),
        dma((offsets + 3,)),
        dma((sends,)),
        dma((others,)),
        dma((others,)),
        dma((others,)),
        dma((others,)),
        dma((rows, chips - 1)),
        dma((rows, chips)),
        dma((chips,)),
        dma((chips - 1,)),
        dma((others,)),
        dma((others,)),
        dma((others,)),
        dma((others,)),
    ]
    whole_vmem = pl.BlockSpec(memory_space=pltpu.VMEM)
    whole_smem = pl.BlockSpec(memory_space=pltpu.SMEM)
    anywhere = pl.BlockSpec(memory_space=pl.ANY)
    return pl.pallas_call(
        functools.partial(kernel, rows, clusters),
        out_shape=[jax.ShapeDtypeStruct((excite, panels), f32)] * 2,
        in_specs=[whole_smem] * 3 + [whole_vmem] * 2 + [anywhere] * 4,
        out_specs=[whole_vmem] * 2,
        scratch_shapes=scratch,
        compiler_params=pltpu.CompilerParams(
            collective_id=0, has_side_effects=True, vmem_limit_bytes=48 * 1024 * 1024
        ),
    )(
        tile_count,
        tile_rows,
        tile_cols,
        excitations,
        adjoint_loads,
        near_tiles,
        skeleton_in,
        skeleton_out,
        kernels,
    )


def solution(mesh):
    clusters, rows = mesh.shape["blk"], mesh.shape["rows"]

    def on_device(*args):
        share = args[8].shape[2]
        tile_size = args[2].shape[1]
        fits = clusters == 8 and rows == 4 and share % 128 == 0
        if fits and tile_size % 128 == 0 and args[2].shape[0] % (2 * GROUP) == 0:
            return tuple(fused_plan(rows, clusters, *args))
        return plain_plan(*args)

    return jax.shard_map(
        on_device,
        mesh=mesh,
        in_specs=(
            P(None, ("blk", "rows")),
            P(None, ("blk", "rows")),
            P(("blk", "rows"), None, None),
            P(("blk", "rows")),
            P(("blk", "rows")),
            P(("blk", "rows")),
            P(None, ("blk", "rows")),
            P(None, ("blk", "rows")),
            P("blk", None, "rows", None),
        ),
        out_specs=(P(None, ("blk", "rows")), P(None, ("blk", "rows"))),
        check_vma=False,
    )
```

```python
import functools

import jax
import jax.numpy as jnp
from jax import lax
from jax.experimental import pallas as pl
from jax.experimental.pallas import tpu as pltpu
from jax.sharding import PartitionSpec as P

highest = lax.Precision.HIGHEST


def plain_plan(
    excitations,
    adjoint_loads,
    near_tiles,
    tile_rows,
    tile_cols,
    tile_count,
    skeleton_in,
    skeleton_out,
    translation,
):
    drive_low = excitations.astype(jnp.bfloat16)
    loads_low = adjoint_loads.astype(jnp.bfloat16)
    excite_count = excitations.shape[0]
    panels = excitations.shape[1]
    tile_size = near_tiles.shape[1]
    kernels = translation[0]
    share_width = kernels.shape[1]
    clusters = lax.axis_size("blk")
    cluster = lax.axis_index("blk")
    gathered = lax.all_gather(drive_low, "rows", axis=1, tiled=True)
    column_blocks = gathered.shape[1] // tile_size
    row_blocks = panels // tile_size
    drive_blocks = gathered.reshape(excite_count, column_blocks, tile_size)
    load_blocks = loads_low.reshape(excite_count, row_blocks, tile_size)
    used_slots = tile_count[0]

    def near_group(group_index, carry):
        ahead, behind = carry
        first_slot = group_index * 4
        tile_group = lax.dynamic_slice_in_dim(near_tiles, first_slot, 4, 0)
        row_ids = lax.dynamic_slice_in_dim(tile_rows, first_slot, 4, 0)
        column_ids = lax.dynamic_slice_in_dim(tile_cols, first_slot, 4, 0)
        live_mask = (first_slot + jnp.arange(4, dtype=jnp.int32) < used_slots).astype(jnp.float32)[
            None, :, None
        ]
        source = jnp.take(drive_blocks, column_ids, axis=1)
        target = jnp.take(load_blocks, row_ids, axis=1)
        forward = (
            jnp.einsum("egj,gij->egi", source, tile_group, preferred_element_type=jnp.float32)
            * live_mask
        )
        backward = (
            jnp.einsum("egi,gij->egj", target, tile_group, preferred_element_type=jnp.float32)
            * live_mask
        )
        return (ahead.at[:, row_ids].add(forward), behind.at[:, column_ids].add(backward))

    near_start = (
        jnp.zeros((excite_count, row_blocks, tile_size), jnp.float32),
        jnp.zeros((excite_count, column_blocks, tile_size), jnp.float32),
    )
    near_ahead, near_behind = lax.fori_loop(0, (used_slots + 3) // 4, near_group, near_start)
    contract_panels = (((1,), (1,)), ((), ()))
    charge_part = lax.dot_general(
        drive_low, skeleton_in, contract_panels, preferred_element_type=jnp.float32
    )
    gradient_part = lax.dot_general(
        loads_low, skeleton_out, contract_panels, preferred_element_type=jnp.float32
    )
    charges, gradient_all = lax.psum((charge_part, gradient_part), "rows")
    gradient = lax.dynamic_slice_in_dim(
        gradient_all, lax.axis_index("rows") * share_width, share_width, 1
    )

    def offsets_for(other_ids):
        offset = jnp.remainder(cluster - other_ids, clusters)
        active = (offset != 0).astype(jnp.float32)
        return (jnp.maximum(offset - 1, 0), active)

    charge_piece = lax.all_gather(charges[None], "blk", axis=0, tiled=True)
    span_count = charge_piece.shape[0]
    offset, active = offsets_for(jnp.arange(span_count, dtype=jnp.int32))
    chosen = jnp.take(kernels, offset, axis=0)
    potential = jnp.einsum(
        "cej,ckj->ek", charge_piece * active[:, None, None], chosen, precision=highest
    )
    potential_low = lax.all_gather(potential.astype(jnp.bfloat16), "rows", axis=1, tiled=True)
    far_ahead = jnp.dot(potential_low, skeleton_out, preferred_element_type=jnp.float32)
    offset, active = offsets_for(jnp.arange(lax.axis_size("blk") * 1, dtype=jnp.int32))
    chosen = jnp.take(kernels, offset, axis=0)
    summed = lax.psum_scatter(
        jnp.einsum("ek,ckj->cej", gradient, chosen, precision=highest) * active[:, None, None],
        "blk",
        scatter_dimension=0,
        tiled=True,
    )
    adjoint_low = lax.psum(summed[0], "rows").astype(jnp.bfloat16)
    far_behind = jnp.dot(adjoint_low, skeleton_in, preferred_element_type=jnp.float32)
    near_columns = lax.psum_scatter(
        near_behind.reshape(excite_count, column_blocks * tile_size),
        "rows",
        scatter_dimension=1,
        tiled=True,
    )
    response = near_ahead.reshape(excite_count, panels) + far_ahead
    sensitivity = near_columns + far_behind
    return (response, sensitivity)


MESH = pl.DeviceIdType.MESH
GROUP = 4
VMEM_BYTES = 62 * 1024 * 1024
bf16 = jnp.bfloat16
f32 = jnp.float32


def dot_nt(a, b):
    return lax.dot_general(a, b, (((1,), (1,)), ((), ())), preferred_element_type=f32)


def dot_nn(a, b):
    return jnp.dot(a, b, preferred_element_type=f32)


def kernel(
    rows,
    clusters,
    count_ref,
    tile_row_hbm,
    tile_col_hbm,
    drive_hbm,
    loads_hbm,
    tiles_hbm,
    skin_hbm,
    skout_hbm,
    trans_hbm,
    response_ref,
    sensitivity_ref,
    tile_row_ref,
    tile_col_ref,
    drive_ref,
    loads_ref,
    tiles,
    skin,
    skout,
    trans,
    trans_low,
    drive_all,
    loads_low,
    grad_part,
    grad_send,
    grad_recv,
    charge_part,
    charge_send,
    charge_recv,
    q_all,
    sib_send,
    sib_recv,
    plane_send,
    plane_recv,
    adj_part,
    adj_send,
    adj_recv,
    adj_all,
    pot_all,
    near_fwd,
    near_adj,
    near_send,
    near_recv,
    local_sem,
    send_sem,
    grad_sem,
    charge_sem,
    drive_sem,
    qz_sem,
    qp_sem,
    qs_sem,
    sib_sem,
    plane_sem,
    adj_sem,
    adjall_sem,
    pot_sem,
    near_sem,
):
    chips = clusters // 2
    b = lax.axis_index("blk")
    r = lax.axis_index("rows")
    core = lax.rem(b, 2)
    chip = lax.div(b, 2)
    cap, size = tiles.shape[0], tiles.shape[1]
    share = q_all.shape[3]
    row_blocks = loads_low.shape[0]
    column_blocks = rows * row_blocks
    offsets = trans.shape[0]

    def row_at(step):
        return lax.rem(r + step + rows, rows)

    def blk_at(step, which):
        return lax.rem(chip + step + chips, chips) * 2 + which

    sibling = b + 1 - 2 * core

    local = []

    def fetch(src, dst):
        copy = pltpu.make_async_copy(src, dst, local_sem.at[len(local)])
        copy.start()
        local.append(copy)
        return copy

    get_loads = fetch(loads_hbm, loads_ref)
    get_out = fetch(skout_hbm, skout)
    get_drive = fetch(drive_hbm, drive_ref)
    get_in = fetch(skin_hbm, skin)
    get_trans = [fetch(trans_hbm.at[d], trans.at[d]) for d in range(offsets)]
    get_tiles = fetch(tiles_hbm, tiles)
    get_lists = [
        fetch(tile_row_hbm, tile_row_ref),
        fetch(tile_col_hbm, tile_col_ref),
    ]

    sent = []

    def send(src, dst, recv, blk, row):
        copy = pltpu.make_async_remote_copy(
            src_ref=src,
            dst_ref=dst,
            send_sem=send_sem.at[len(sent)],
            recv_sem=recv,
            device_id=(blk, row),
            device_id_type=MESH,
        )
        copy.start()
        sent.append(copy)
        return copy

    barrier = pltpu.get_barrier_semaphore()
    partners = [(b, row_at(o)) for o in range(1, rows)]
    partners += [(blk_at(o, core), r) for o in range(1, chips)]
    partners += [(sibling, r)]
    for partner in partners:
        pl.semaphore_signal(barrier, inc=1, device_id=partner, device_id_type=MESH)

    get_loads.wait()
    for i in range(row_blocks):
        loads_low[i] = loads_ref[:, i * size : (i + 1) * size].astype(bf16)
    loads_wide = loads_ref[...].astype(bf16)
    get_out.wait()
    for j in range(rows):
        part = dot_nt(loads_wide, skout[j * share : (j + 1) * share, :])
        grad_part[j] = part
        grad_send[j] = part.astype(bf16)
    pl.semaphore_wait(barrier, len(partners))
    grad_copies = [
        send(grad_send.at[row_at(o)], grad_recv.at[o - 1], grad_sem.at[o - 1], b, row_at(o))
        for o in range(1, rows)
    ]
    get_drive.wait()
    for i in range(row_blocks):
        drive_all[r * row_blocks + i] = drive_ref[:, i * size : (i + 1) * size].astype(bf16)
    drive_wide = drive_ref[...].astype(bf16)
    get_in.wait()
    for j in range(rows):
        part = dot_nt(drive_wide, skin[j * share : (j + 1) * share, :])
        charge_part[j] = part
        charge_send[j] = part.astype(bf16)
    charge_copies = [
        send(charge_send.at[row_at(o)], charge_recv.at[o - 1], charge_sem.at[o - 1], b, row_at(o))
        for o in range(1, rows)
    ]

    for d in range(offsets):
        get_trans[d].wait()
        trans_low[d] = trans[d].astype(bf16)

    for copy in grad_copies:
        copy.wait_recv()
    gradient = grad_part[r]
    for o in range(rows - 1):
        gradient += grad_recv[o].astype(f32)
    grad_high = gradient.astype(bf16)
    grad_rest = (gradient - grad_high.astype(f32)).astype(bf16)
    grad_both = jnp.concatenate([grad_high, grad_rest], axis=0)
    excite = gradient.shape[0]

    for copy in charge_copies:
        copy.wait_recv()
    charge = charge_part[r]
    for o in range(rows - 1):
        charge += charge_recv[o].astype(f32)
    q_all[r, b] = charge.astype(bf16)

    def send_quarter_to_plane(z):
        piece = q_all.at[row_at(-z), b]
        copies = [
            send(piece, piece, qp_sem.at[z, o - 1], blk_at(o, core), r) for o in range(1, chips)
        ]
        return copies, [send(piece, piece, qs_sem.at[z, 0], sibling, r)]

    piece = q_all.at[r, b]
    qz_copies = [send(piece, piece, qz_sem.at[o - 1], b, row_at(o)) for o in range(1, rows)]
    plane_q, sibling_q = [None] * rows, [None] * rows
    plane_q[0], sibling_q[0] = send_quarter_to_plane(0)

    mine = pl.ds(r * row_blocks, row_blocks)
    drive_copies = [
        send(drive_all.at[mine], drive_all.at[mine], drive_sem.at[o - 1], b, row_at(o))
        for o in range(1, rows)
    ]

    def adjoint_term(target, j):
        index = lax.rem(b - target + clusters, clusters) - 1
        both = dot_nn(grad_both, trans_low[index, :, j * share : (j + 1) * share])
        return both[:excite] + both[excite:]

    sib_copies = []
    for o in range(chips):
        for j in range(rows):
            sib_send[o, j] = adjoint_term(blk_at(o, 1 - core), j).astype(bf16)
        sib_copies.append(send(sib_send.at[o], sib_recv.at[o], sib_sem.at[o], sibling, r))
    for z in range(1, rows):
        qz_copies[z - 1].wait_recv()
        plane_q[z], sibling_q[z] = send_quarter_to_plane(z)
    plane_copies = []
    for o in range(1, chips):
        terms = [adjoint_term(blk_at(o, core), j) for j in range(rows)]
        sib_copies[o].wait_recv()
        for j in range(rows):
            plane_send[o - 1, j] = (terms[j] + sib_recv[o, j].astype(f32)).astype(bf16)
        plane_copies.append(
            send(
                plane_send.at[o - 1],
                plane_recv.at[o - 1],
                plane_sem.at[o - 1],
                blk_at(o, core),
                r,
            )
        )

    near_adj[...] = jnp.zeros_like(near_adj)
    near_fwd[...] = jnp.zeros_like(near_fwd)
    get_tiles.wait()
    for copy in get_lists:
        copy.wait()

    used = count_ref[0]

    def adjoint_group(group, carry):
        products, columns = [], []
        for t in range(GROUP):
            slot = group * GROUP + t
            source = loads_low[tile_row_ref[slot]]
            products.append(dot_nn(source, tiles[slot]))
            columns.append(jnp.where(slot < used, tile_col_ref[slot], -1))
        for c in range(column_blocks):
            total = near_adj[c]
            for t in range(GROUP):
                total += products[t] * jnp.where(columns[t] == c, 1.0, 0.0).astype(f32)
            near_adj[c] = total
        return carry

    def forward_group(group, carry):
        products, targets = [], []
        for t in range(GROUP):
            slot = group * GROUP + t
            source = drive_all[tile_col_ref[slot]]
            products.append(dot_nt(source, tiles[slot]))
            targets.append(jnp.where(slot < used, tile_row_ref[slot], -1))
        for i in range(row_blocks):
            total = near_fwd[i]
            for t in range(GROUP):
                total += products[t] * jnp.where(targets[t] == i, 1.0, 0.0).astype(f32)
            near_fwd[i] = total
        return carry

    groups = cap // GROUP
    lax.fori_loop(0, groups, adjoint_group, 0)
    for c in range(column_blocks):
        near_send[c] = near_adj[c].astype(bf16)
    near_copies = [
        send(
            near_send.at[pl.ds(row_at(o) * row_blocks, row_blocks)],
            near_recv.at[o - 1],
            near_sem.at[o - 1],
            b,
            row_at(o),
        )
        for o in range(1, rows)
    ]

    for z in range(rows):
        for o in range(1, chips):
            plane_q[z][o - 1].wait_recv()
            piece = q_all.at[row_at(-z), blk_at(-o, core)]
            sibling_q[z].append(send(piece, piece, qs_sem.at[z, o], sibling, r))

    for copy in drive_copies:
        copy.wait_recv()
    lax.fori_loop(0, groups // 4, forward_group, 0)

    for z in range(rows):
        for copy in sibling_q[z]:
            copy.wait_recv()
    potential = jnp.zeros((excite, share), f32)
    for j in range(rows):
        for d in range(1, offsets + 1):
            source = q_all[j, lax.rem(b - d + clusters, clusters)]
            potential += dot_nt(source, trans_low[d - 1, :, j * share : (j + 1) * share])
    pot_all[r] = potential.astype(bf16)
    piece = pot_all.at[r]
    pot_copies = [send(piece, piece, pot_sem.at[o - 1], b, row_at(o)) for o in range(1, rows)]

    sib_copies[0].wait_recv()
    for copy in plane_copies:
        copy.wait_recv()
    for j in range(rows):
        total = sib_recv[0, j].astype(f32)
        for o in range(chips - 1):
            total += plane_recv[o, j].astype(f32)
        adj_part[j] = total
        adj_send[j] = total.astype(bf16)
    adj_copies = [
        send(adj_send.at[row_at(o)], adj_recv.at[o - 1], adj_sem.at[o - 1], b, row_at(o))
        for o in range(1, rows)
    ]

    lax.fori_loop(groups // 4, groups // 4 * 3, forward_group, 0)

    for copy in adj_copies:
        copy.wait_recv()
    adjoint = adj_part[r]
    for o in range(rows - 1):
        adjoint += adj_recv[o].astype(f32)
    adj_all[r] = adjoint.astype(bf16)
    piece = adj_all.at[r]
    adjall_copies = [send(piece, piece, adjall_sem.at[o - 1], b, row_at(o)) for o in range(1, rows)]

    lax.fori_loop(groups // 4 * 3, groups, forward_group, 0)

    for copy in near_copies:
        copy.wait_recv()
    for i in range(row_blocks):
        total = near_adj[r * row_blocks + i]
        for o in range(rows - 1):
            total += near_recv[o, i].astype(f32)
        near_adj[r * row_blocks + i] = total

    for copy in pot_copies:
        copy.wait_recv()
    for i in range(row_blocks):
        total = near_fwd[i]
        for j in range(rows):
            block = skout[j * share : (j + 1) * share, i * size : (i + 1) * size]
            total += dot_nn(pot_all[j], block)
        response_ref[:, i * size : (i + 1) * size] = total
    for copy in adjall_copies:
        copy.wait_recv()
    for i in range(row_blocks):
        total = near_adj[r * row_blocks + i]
        for j in range(rows):
            block = skin[j * share : (j + 1) * share, i * size : (i + 1) * size]
            total += dot_nn(adj_all[j], block)
        sensitivity_ref[:, i * size : (i + 1) * size] = total
    for copy in sent:
        copy.wait_send()


def fused_plan(
    rows,
    clusters,
    excitations,
    adjoint_loads,
    near_tiles,
    tile_rows,
    tile_cols,
    tile_count,
    skeleton_in,
    skeleton_out,
    translation,
):
    kernels = translation[0]
    excite, panels = excitations.shape
    cap, size = near_tiles.shape[:2]
    offsets, share, points = kernels.shape
    chips = clusters // 2
    row_blocks = panels // size
    blocks = rows * row_blocks
    others = rows - 1
    sends = 7 * others + rows * (chips - 1) + rows * chips + chips + chips - 1 + others
    vmem, dma = pltpu.VMEM, pltpu.SemaphoreType.DMA
    scratch = [
        pltpu.SMEM(tile_rows.shape, jnp.int32),
        pltpu.SMEM(tile_cols.shape, jnp.int32),
        vmem((excite, panels), f32),
        vmem((excite, panels), f32),
        vmem((cap, size, size), bf16),
        vmem((points, panels), bf16),
        vmem((points, panels), bf16),
        vmem((offsets, share, points), f32),
        vmem((offsets, share, points), bf16),
        vmem((blocks, excite, size), bf16),
        vmem((row_blocks, excite, size), bf16),
        vmem((rows, excite, share), f32),
        vmem((rows, excite, share), bf16),
        vmem((others, excite, share), bf16),
        vmem((rows, excite, share), f32),
        vmem((rows, excite, share), bf16),
        vmem((others, excite, share), bf16),
        vmem((rows, clusters, excite, share), bf16),
        vmem((chips, rows, excite, share), bf16),
        vmem((chips, rows, excite, share), bf16),
        vmem((chips - 1, rows, excite, share), bf16),
        vmem((chips - 1, rows, excite, share), bf16),
        vmem((rows, excite, share), f32),
        vmem((rows, excite, share), bf16),
        vmem((others, excite, share), bf16),
        vmem((rows, excite, share), bf16),
        vmem((rows, excite, share), bf16),
        vmem((row_blocks, excite, size), f32),
        vmem((blocks, excite, size), f32),
        vmem((blocks, excite, size), bf16),
        vmem((others, row_blocks, excite, size), bf16),
        dma((offsets + 7,)),
        dma((sends,)),
        dma((others,)),
        dma((others,)),
        dma((others,)),
        dma((others,)),
        dma((rows, chips - 1)),
        dma((rows, chips)),
        dma((chips,)),
        dma((chips - 1,)),
        dma((others,)),
        dma((others,)),
        dma((others,)),
        dma((others,)),
    ]
    whole_vmem = pl.BlockSpec(memory_space=pltpu.VMEM)
    anywhere = pl.BlockSpec(memory_space=pl.ANY)
    return pl.pallas_call(
        functools.partial(kernel, rows, clusters),
        out_shape=[jax.ShapeDtypeStruct((excite, panels), f32)] * 2,
        in_specs=[pl.BlockSpec(memory_space=pltpu.SMEM)] + [anywhere] * 8,
        out_specs=[whole_vmem] * 2,
        scratch_shapes=scratch,
        compiler_params=pltpu.CompilerParams(
            collective_id=0, has_side_effects=True, vmem_limit_bytes=VMEM_BYTES
        ),
    )(
        tile_count,
        tile_rows,
        tile_cols,
        excitations,
        adjoint_loads,
        near_tiles,
        skeleton_in,
        skeleton_out,
        kernels,
    )


def solution(mesh):
    clusters, rows = mesh.shape["blk"], mesh.shape["rows"]

    def on_device(*args):
        share = args[8].shape[2]
        tile_size = args[2].shape[1]
        fits = clusters == 8 and rows == 4 and share % 128 == 0
        if fits and tile_size % 128 == 0 and args[2].shape[0] % (2 * GROUP) == 0:
            return tuple(fused_plan(rows, clusters, *args))
        return plain_plan(*args)

    return jax.shard_map(
        on_device,
        mesh=mesh,
        in_specs=(
            P(None, ("blk", "rows")),
            P(None, ("blk", "rows")),
            P(("blk", "rows"), None, None),
            P(("blk", "rows")),
            P(("blk", "rows")),
            P(("blk", "rows")),
            P(None, ("blk", "rows")),
            P(None, ("blk", "rows")),
            P("blk", None, "rows", None),
        ),
        out_specs=(P(None, ("blk", "rows")), P(None, ("blk", "rows"))),
        check_vma=False,
    )
```

```python
import functools

import jax
import jax.numpy as jnp
from jax import lax
from jax.experimental import pallas as pl
from jax.experimental.pallas import tpu as pltpu
from jax.sharding import PartitionSpec as P

highest = lax.Precision.HIGHEST


def plain_plan(
    excitations,
    adjoint_loads,
    near_tiles,
    tile_rows,
    tile_cols,
    tile_count,
    skeleton_in,
    skeleton_out,
    translation,
):
    drive_low = excitations.astype(jnp.bfloat16)
    loads_low = adjoint_loads.astype(jnp.bfloat16)
    excite_count = excitations.shape[0]
    panels = excitations.shape[1]
    tile_size = near_tiles.shape[1]
    kernels = translation[0]
    share_width = kernels.shape[1]
    clusters = lax.axis_size("blk")
    cluster = lax.axis_index("blk")
    gathered = lax.all_gather(drive_low, "rows", axis=1, tiled=True)
    column_blocks = gathered.shape[1] // tile_size
    row_blocks = panels // tile_size
    drive_blocks = gathered.reshape(excite_count, column_blocks, tile_size)
    load_blocks = loads_low.reshape(excite_count, row_blocks, tile_size)
    used_slots = tile_count[0]

    def near_group(group_index, carry):
        ahead, behind = carry
        first_slot = group_index * 4
        tile_group = lax.dynamic_slice_in_dim(near_tiles, first_slot, 4, 0)
        row_ids = lax.dynamic_slice_in_dim(tile_rows, first_slot, 4, 0)
        column_ids = lax.dynamic_slice_in_dim(tile_cols, first_slot, 4, 0)
        live_mask = (first_slot + jnp.arange(4, dtype=jnp.int32) < used_slots).astype(jnp.float32)[
            None, :, None
        ]
        source = jnp.take(drive_blocks, column_ids, axis=1)
        target = jnp.take(load_blocks, row_ids, axis=1)
        forward = (
            jnp.einsum("egj,gij->egi", source, tile_group, preferred_element_type=jnp.float32)
            * live_mask
        )
        backward = (
            jnp.einsum("egi,gij->egj", target, tile_group, preferred_element_type=jnp.float32)
            * live_mask
        )
        return (ahead.at[:, row_ids].add(forward), behind.at[:, column_ids].add(backward))

    near_start = (
        jnp.zeros((excite_count, row_blocks, tile_size), jnp.float32),
        jnp.zeros((excite_count, column_blocks, tile_size), jnp.float32),
    )
    near_ahead, near_behind = lax.fori_loop(0, (used_slots + 3) // 4, near_group, near_start)
    contract_panels = (((1,), (1,)), ((), ()))
    charge_part = lax.dot_general(
        drive_low, skeleton_in, contract_panels, preferred_element_type=jnp.float32
    )
    gradient_part = lax.dot_general(
        loads_low, skeleton_out, contract_panels, preferred_element_type=jnp.float32
    )
    charges, gradient_all = lax.psum((charge_part, gradient_part), "rows")
    gradient = lax.dynamic_slice_in_dim(
        gradient_all, lax.axis_index("rows") * share_width, share_width, 1
    )

    def offsets_for(other_ids):
        offset = jnp.remainder(cluster - other_ids, clusters)
        active = (offset != 0).astype(jnp.float32)
        return (jnp.maximum(offset - 1, 0), active)

    charge_piece = lax.all_gather(charges[None], "blk", axis=0, tiled=True)
    span_count = charge_piece.shape[0]
    offset, active = offsets_for(jnp.arange(span_count, dtype=jnp.int32))
    chosen = jnp.take(kernels, offset, axis=0)
    potential = jnp.einsum(
        "cej,ckj->ek", charge_piece * active[:, None, None], chosen, precision=highest
    )
    potential_low = lax.all_gather(potential.astype(jnp.bfloat16), "rows", axis=1, tiled=True)
    far_ahead = jnp.dot(potential_low, skeleton_out, preferred_element_type=jnp.float32)
    offset, active = offsets_for(jnp.arange(lax.axis_size("blk") * 1, dtype=jnp.int32))
    chosen = jnp.take(kernels, offset, axis=0)
    summed = lax.psum_scatter(
        jnp.einsum("ek,ckj->cej", gradient, chosen, precision=highest) * active[:, None, None],
        "blk",
        scatter_dimension=0,
        tiled=True,
    )
    adjoint_low = lax.psum(summed[0], "rows").astype(jnp.bfloat16)
    far_behind = jnp.dot(adjoint_low, skeleton_in, preferred_element_type=jnp.float32)
    near_columns = lax.psum_scatter(
        near_behind.reshape(excite_count, column_blocks * tile_size),
        "rows",
        scatter_dimension=1,
        tiled=True,
    )
    response = near_ahead.reshape(excite_count, panels) + far_ahead
    sensitivity = near_columns + far_behind
    return (response, sensitivity)


MESH = pl.DeviceIdType.MESH
GROUP = 4
VMEM_BYTES = 62 * 1024 * 1024
bf16 = jnp.bfloat16
f32 = jnp.float32


def dot_nt(a, b):
    return lax.dot_general(a, b, (((1,), (1,)), ((), ())), preferred_element_type=f32)


def dot_nn(a, b):
    return jnp.dot(a, b, preferred_element_type=f32)


def kernel(
    rows,
    clusters,
    count_ref,
    tile_row_hbm,
    tile_col_hbm,
    drive_hbm,
    loads_hbm,
    tiles_hbm,
    skin_hbm,
    skout_hbm,
    trans_hbm,
    response_hbm,
    sensitivity_hbm,
    response_ref,
    sensitivity_ref,
    tile_row_ref,
    tile_col_ref,
    drive_ref,
    loads_ref,
    tiles,
    skin,
    skout,
    trans,
    trans_low,
    drive_all,
    loads_low,
    grad_part,
    grad_send,
    grad_recv,
    charge_part,
    charge_send,
    charge_recv,
    q_all,
    sib_send,
    sib_recv,
    plane_send,
    plane_recv,
    adj_part,
    adj_send,
    adj_recv,
    adj_all,
    pot_all,
    near_fwd,
    near_adj,
    near_send,
    near_recv,
    local_sem,
    send_sem,
    grad_sem,
    charge_sem,
    drive_sem,
    qz_sem,
    qp_sem,
    qs_sem,
    sib_sem,
    plane_sem,
    adj_sem,
    adjall_sem,
    pot_sem,
    near_sem,
):
    chips = clusters // 2
    b = lax.axis_index("blk")
    r = lax.axis_index("rows")
    core = lax.rem(b, 2)
    chip = lax.div(b, 2)
    cap, size = tiles.shape[0], tiles.shape[1]
    share = q_all.shape[3]
    row_blocks = loads_low.shape[0]
    column_blocks = rows * row_blocks
    offsets = trans.shape[0]

    def row_at(step):
        return lax.rem(r + step + rows, rows)

    def blk_at(step, which):
        return lax.rem(chip + step + chips, chips) * 2 + which

    sibling = b + 1 - 2 * core

    local = []

    def fetch(src, dst):
        copy = pltpu.make_async_copy(src, dst, local_sem.at[len(local)])
        copy.start()
        local.append(copy)
        return copy

    get_loads = fetch(loads_hbm, loads_ref)
    get_out = fetch(skout_hbm, skout)
    get_drive = fetch(drive_hbm, drive_ref)
    get_in = fetch(skin_hbm, skin)
    get_trans = [fetch(trans_hbm.at[d], trans.at[d]) for d in range(offsets)]
    get_tiles = fetch(tiles_hbm, tiles)
    get_lists = [
        fetch(tile_row_hbm, tile_row_ref),
        fetch(tile_col_hbm, tile_col_ref),
    ]

    sent = []

    def send(src, dst, recv, blk, row):
        copy = pltpu.make_async_remote_copy(
            src_ref=src,
            dst_ref=dst,
            send_sem=send_sem.at[len(sent)],
            recv_sem=recv,
            device_id=(blk, row),
            device_id_type=MESH,
        )
        copy.start()
        sent.append(copy)
        return copy

    barrier = pltpu.get_barrier_semaphore()
    partners = [(b, row_at(o)) for o in range(1, rows)]
    partners += [(blk_at(o, core), r) for o in range(1, chips)]
    partners += [(sibling, r)]
    for partner in partners:
        pl.semaphore_signal(barrier, inc=1, device_id=partner, device_id_type=MESH)

    get_loads.wait()
    for i in range(row_blocks):
        loads_low[i] = loads_ref[:, i * size : (i + 1) * size].astype(bf16)
    loads_wide = loads_ref[...].astype(bf16)
    get_out.wait()
    for j in range(rows):
        part = dot_nt(loads_wide, skout[j * share : (j + 1) * share, :])
        grad_part[j] = part
        grad_send[j] = part.astype(bf16)
    pl.semaphore_wait(barrier, len(partners))
    grad_copies = [
        send(grad_send.at[row_at(o)], grad_recv.at[o - 1], grad_sem.at[o - 1], b, row_at(o))
        for o in range(1, rows)
    ]
    get_drive.wait()
    for i in range(row_blocks):
        drive_all[r * row_blocks + i] = drive_ref[:, i * size : (i + 1) * size].astype(bf16)
    drive_wide = drive_ref[...].astype(bf16)
    get_in.wait()
    for j in range(rows):
        part = dot_nt(drive_wide, skin[j * share : (j + 1) * share, :])
        charge_part[j] = part
        charge_send[j] = part.astype(bf16)
    charge_copies = [
        send(charge_send.at[row_at(o)], charge_recv.at[o - 1], charge_sem.at[o - 1], b, row_at(o))
        for o in range(1, rows)
    ]

    for d in range(offsets):
        get_trans[d].wait()
        trans_low[d] = trans[d].astype(bf16)

    for copy in grad_copies:
        copy.wait_recv()
    gradient = grad_part[r]
    for o in range(rows - 1):
        gradient += grad_recv[o].astype(f32)
    grad_high = gradient.astype(bf16)
    grad_rest = (gradient - grad_high.astype(f32)).astype(bf16)
    grad_both = jnp.concatenate([grad_high, grad_rest], axis=0)
    excite = gradient.shape[0]

    def adjoint_term(target, j):
        index = lax.rem(b - target + clusters, clusters) - 1
        both = dot_nn(grad_both, trans_low[index, :, j * share : (j + 1) * share])
        return both[:excite] + both[excite:]

    sib_copies = []
    for o in range(chips):
        for j in range(rows):
            sib_send[o, j] = adjoint_term(blk_at(o, 1 - core), j).astype(bf16)
        sib_copies.append(send(sib_send.at[o], sib_recv.at[o], sib_sem.at[o], sibling, r))

    for copy in charge_copies:
        copy.wait_recv()
    charge = charge_part[r]
    for o in range(rows - 1):
        charge += charge_recv[o].astype(f32)
    q_all[r, b] = charge.astype(bf16)

    def send_quarter_to_plane(z):
        piece = q_all.at[row_at(-z), b]
        copies = [
            send(piece, piece, qp_sem.at[z, o - 1], blk_at(o, core), r) for o in range(1, chips)
        ]
        return copies, [send(piece, piece, qs_sem.at[z, 0], sibling, r)]

    piece = q_all.at[r, b]
    qz_copies = [send(piece, piece, qz_sem.at[o - 1], b, row_at(o)) for o in range(1, rows)]
    plane_q, sibling_q = [None] * rows, [None] * rows
    plane_q[0], sibling_q[0] = send_quarter_to_plane(0)

    mine = pl.ds(r * row_blocks, row_blocks)
    drive_copies = [
        send(drive_all.at[mine], drive_all.at[mine], drive_sem.at[o - 1], b, row_at(o))
        for o in range(1, rows)
    ]

    plane_copies = []
    for o in range(1, chips):
        terms = [adjoint_term(blk_at(o, core), j) for j in range(rows)]
        sib_copies[o].wait_recv()
        for j in range(rows):
            plane_send[o - 1, j] = (terms[j] + sib_recv[o, j].astype(f32)).astype(bf16)
        plane_copies.append(
            send(
                plane_send.at[o - 1],
                plane_recv.at[o - 1],
                plane_sem.at[o - 1],
                blk_at(o, core),
                r,
            )
        )

    for z in range(1, rows):
        qz_copies[z - 1].wait_recv()
        plane_q[z], sibling_q[z] = send_quarter_to_plane(z)

    near_adj[...] = jnp.zeros_like(near_adj)
    near_fwd[...] = jnp.zeros_like(near_fwd)
    get_tiles.wait()
    for copy in get_lists:
        copy.wait()

    used = count_ref[0]

    def adjoint_group(group, carry):
        products, columns = [], []
        for t in range(GROUP):
            slot = group * GROUP + t
            source = loads_low[tile_row_ref[slot]]
            products.append(dot_nn(source, tiles[slot]))
            columns.append(jnp.where(slot < used, tile_col_ref[slot], -1))
        for c in range(column_blocks):
            total = near_adj[c]
            for t in range(GROUP):
                total += products[t] * jnp.where(columns[t] == c, 1.0, 0.0).astype(f32)
            near_adj[c] = total
        return carry

    def forward_group(group, carry):
        products, targets = [], []
        for t in range(GROUP):
            slot = group * GROUP + t
            source = drive_all[tile_col_ref[slot]]
            products.append(dot_nt(source, tiles[slot]))
            targets.append(jnp.where(slot < used, tile_row_ref[slot], -1))
        for i in range(row_blocks):
            total = near_fwd[i]
            for t in range(GROUP):
                total += products[t] * jnp.where(targets[t] == i, 1.0, 0.0).astype(f32)
            near_fwd[i] = total
        return carry

    groups = cap // GROUP
    lax.fori_loop(0, groups, adjoint_group, 0)
    sib_copies[0].wait_recv()
    for copy in plane_copies:
        copy.wait_recv()
    for j in range(rows):
        total = sib_recv[0, j].astype(f32)
        for o in range(chips - 1):
            total += plane_recv[o, j].astype(f32)
        adj_part[j] = total
        adj_send[j] = total.astype(bf16)
    adj_copies = [
        send(adj_send.at[row_at(o)], adj_recv.at[o - 1], adj_sem.at[o - 1], b, row_at(o))
        for o in range(1, rows)
    ]

    for c in range(column_blocks):
        near_send[c] = near_adj[c].astype(bf16)
    near_copies = [
        send(
            near_send.at[pl.ds(row_at(o) * row_blocks, row_blocks)],
            near_recv.at[o - 1],
            near_sem.at[o - 1],
            b,
            row_at(o),
        )
        for o in range(1, rows)
    ]

    for z in range(rows):
        for o in range(1, chips):
            plane_q[z][o - 1].wait_recv()
            piece = q_all.at[row_at(-z), blk_at(-o, core)]
            sibling_q[z].append(send(piece, piece, qs_sem.at[z, o], sibling, r))

    for copy in drive_copies:
        copy.wait_recv()
    lax.fori_loop(0, groups // 2, forward_group, 0)

    for copy in adj_copies:
        copy.wait_recv()
    adjoint = adj_part[r]
    for o in range(rows - 1):
        adjoint += adj_recv[o].astype(f32)
    adj_all[r] = adjoint.astype(bf16)
    piece = adj_all.at[r]
    adjall_copies = [send(piece, piece, adjall_sem.at[o - 1], b, row_at(o)) for o in range(1, rows)]

    for z in range(rows):
        for copy in sibling_q[z]:
            copy.wait_recv()
    potential = jnp.zeros((excite, share), f32)
    for j in range(rows):
        for d in range(1, offsets + 1):
            source = q_all[j, lax.rem(b - d + clusters, clusters)]
            potential += dot_nt(source, trans_low[d - 1, :, j * share : (j + 1) * share])
    pot_all[r] = potential.astype(bf16)
    piece = pot_all.at[r]
    pot_copies = [send(piece, piece, pot_sem.at[o - 1], b, row_at(o)) for o in range(1, rows)]

    lax.fori_loop(groups // 2, groups, forward_group, 0)

    for copy in near_copies:
        copy.wait_recv()
    for i in range(row_blocks):
        total = near_adj[r * row_blocks + i]
        for o in range(rows - 1):
            total += near_recv[o, i].astype(f32)
        near_adj[r * row_blocks + i] = total

    for copy in pot_copies:
        copy.wait_recv()
    for i in range(row_blocks):
        total = near_fwd[i]
        for j in range(rows):
            block = skout[j * share : (j + 1) * share, i * size : (i + 1) * size]
            total += dot_nn(pot_all[j], block)
        response_ref[:, i * size : (i + 1) * size] = total
    put_response = fetch(response_ref, response_hbm)
    for copy in adjall_copies:
        copy.wait_recv()
    for i in range(row_blocks):
        total = near_adj[r * row_blocks + i]
        for j in range(rows):
            block = skin[j * share : (j + 1) * share, i * size : (i + 1) * size]
            total += dot_nn(adj_all[j], block)
        sensitivity_ref[:, i * size : (i + 1) * size] = total
    put_sensitivity = fetch(sensitivity_ref, sensitivity_hbm)
    for copy in sent:
        copy.wait_send()
    put_response.wait()
    put_sensitivity.wait()


def landing(response, sensitivity, response_out, sensitivity_out, sem):
    copies = [
        pltpu.make_async_copy(response, response_out, sem.at[0]),
        pltpu.make_async_copy(sensitivity, sensitivity_out, sem.at[1]),
    ]
    for copy in copies:
        copy.start()
    for copy in copies:
        copy.wait()


def fused_plan(
    rows,
    clusters,
    excitations,
    adjoint_loads,
    near_tiles,
    tile_rows,
    tile_cols,
    tile_count,
    skeleton_in,
    skeleton_out,
    translation,
):
    kernels = translation[0]
    excite, panels = excitations.shape
    cap, size = near_tiles.shape[:2]
    offsets, share, points = kernels.shape
    chips = clusters // 2
    row_blocks = panels // size
    blocks = rows * row_blocks
    others = rows - 1
    sends = 7 * others + rows * (chips - 1) + rows * chips + chips + chips - 1 + others
    vmem, dma = pltpu.VMEM, pltpu.SemaphoreType.DMA
    scratch = [
        vmem((excite, panels), f32),
        vmem((excite, panels), f32),
        pltpu.SMEM(tile_rows.shape, jnp.int32),
        pltpu.SMEM(tile_cols.shape, jnp.int32),
        vmem((excite, panels), f32),
        vmem((excite, panels), f32),
        vmem((cap, size, size), bf16),
        vmem((points, panels), bf16),
        vmem((points, panels), bf16),
        vmem((offsets, share, points), f32),
        vmem((offsets, share, points), bf16),
        vmem((blocks, excite, size), bf16),
        vmem((row_blocks, excite, size), bf16),
        vmem((rows, excite, share), f32),
        vmem((rows, excite, share), bf16),
        vmem((others, excite, share), bf16),
        vmem((rows, excite, share), f32),
        vmem((rows, excite, share), bf16),
        vmem((others, excite, share), bf16),
        vmem((rows, clusters, excite, share), bf16),
        vmem((chips, rows, excite, share), bf16),
        vmem((chips, rows, excite, share), bf16),
        vmem((chips - 1, rows, excite, share), bf16),
        vmem((chips - 1, rows, excite, share), bf16),
        vmem((rows, excite, share), f32),
        vmem((rows, excite, share), bf16),
        vmem((others, excite, share), bf16),
        vmem((rows, excite, share), bf16),
        vmem((rows, excite, share), bf16),
        vmem((row_blocks, excite, size), f32),
        vmem((blocks, excite, size), f32),
        vmem((blocks, excite, size), bf16),
        vmem((others, row_blocks, excite, size), bf16),
        dma((offsets + 9,)),
        dma((sends,)),
        dma((others,)),
        dma((others,)),
        dma((others,)),
        dma((others,)),
        dma((rows, chips - 1)),
        dma((rows, chips)),
        dma((chips,)),
        dma((chips - 1,)),
        dma((others,)),
        dma((others,)),
        dma((others,)),
        dma((others,)),
    ]
    anywhere = pl.BlockSpec(memory_space=pl.ANY)
    results = pl.pallas_call(
        functools.partial(kernel, rows, clusters),
        out_shape=[jax.ShapeDtypeStruct((excite, panels), f32)] * 2,
        in_specs=[pl.BlockSpec(memory_space=pltpu.SMEM)] + [anywhere] * 8,
        out_specs=[anywhere] * 2,
        scratch_shapes=scratch,
        compiler_params=pltpu.CompilerParams(
            collective_id=0, has_side_effects=True, vmem_limit_bytes=VMEM_BYTES
        ),
    )(
        tile_count,
        tile_rows,
        tile_cols,
        excitations,
        adjoint_loads,
        near_tiles,
        skeleton_in,
        skeleton_out,
        kernels,
    )
    return pl.pallas_call(
        landing,
        out_shape=[jax.ShapeDtypeStruct((excite, panels), f32)] * 2,
        in_specs=[anywhere] * 2,
        out_specs=[anywhere] * 2,
        scratch_shapes=[dma((2,))],
        compiler_params=pltpu.CompilerParams(vmem_limit_bytes=VMEM_BYTES),
    )(*results)


def solution(mesh):
    clusters, rows = mesh.shape["blk"], mesh.shape["rows"]

    def on_device(*args):
        share = args[8].shape[2]
        tile_size = args[2].shape[1]
        fits = clusters == 8 and rows == 4 and share % 128 == 0
        if fits and tile_size % 128 == 0 and args[2].shape[0] % (2 * GROUP) == 0:
            return tuple(fused_plan(rows, clusters, *args))
        return plain_plan(*args)

    return jax.shard_map(
        on_device,
        mesh=mesh,
        in_specs=(
            P(None, ("blk", "rows")),
            P(None, ("blk", "rows")),
            P(("blk", "rows"), None, None),
            P(("blk", "rows")),
            P(("blk", "rows")),
            P(("blk", "rows")),
            P(None, ("blk", "rows")),
            P(None, ("blk", "rows")),
            P("blk", None, "rows", None),
        ),
        out_specs=(P(None, ("blk", "rows")), P(None, ("blk", "rows"))),
        check_vma=False,
    )
```

```python
import functools

import jax
import jax.numpy as jnp
from jax import lax
from jax.experimental import pallas as pl
from jax.experimental.pallas import tpu as pltpu
from jax.sharding import PartitionSpec as P

highest = lax.Precision.HIGHEST


def plain_plan(
    excitations,
    adjoint_loads,
    near_tiles,
    tile_rows,
    tile_cols,
    tile_count,
    skeleton_in,
    skeleton_out,
    translation,
):
    drive_low = excitations.astype(jnp.bfloat16)
    loads_low = adjoint_loads.astype(jnp.bfloat16)
    excite_count = excitations.shape[0]
    panels = excitations.shape[1]
    tile_size = near_tiles.shape[1]
    kernels = translation[0]
    share_width = kernels.shape[1]
    clusters = lax.axis_size("blk")
    cluster = lax.axis_index("blk")
    gathered = lax.all_gather(drive_low, "rows", axis=1, tiled=True)
    column_blocks = gathered.shape[1] // tile_size
    row_blocks = panels // tile_size
    drive_blocks = gathered.reshape(excite_count, column_blocks, tile_size)
    load_blocks = loads_low.reshape(excite_count, row_blocks, tile_size)
    used_slots = tile_count[0]

    def near_group(group_index, carry):
        ahead, behind = carry
        first_slot = group_index * 4
        tile_group = lax.dynamic_slice_in_dim(near_tiles, first_slot, 4, 0)
        row_ids = lax.dynamic_slice_in_dim(tile_rows, first_slot, 4, 0)
        column_ids = lax.dynamic_slice_in_dim(tile_cols, first_slot, 4, 0)
        live_mask = (first_slot + jnp.arange(4, dtype=jnp.int32) < used_slots).astype(jnp.float32)[
            None, :, None
        ]
        source = jnp.take(drive_blocks, column_ids, axis=1)
        target = jnp.take(load_blocks, row_ids, axis=1)
        forward = (
            jnp.einsum("egj,gij->egi", source, tile_group, preferred_element_type=jnp.float32)
            * live_mask
        )
        backward = (
            jnp.einsum("egi,gij->egj", target, tile_group, preferred_element_type=jnp.float32)
            * live_mask
        )
        return (ahead.at[:, row_ids].add(forward), behind.at[:, column_ids].add(backward))

    near_start = (
        jnp.zeros((excite_count, row_blocks, tile_size), jnp.float32),
        jnp.zeros((excite_count, column_blocks, tile_size), jnp.float32),
    )
    near_ahead, near_behind = lax.fori_loop(0, (used_slots + 3) // 4, near_group, near_start)
    contract_panels = (((1,), (1,)), ((), ()))
    charge_part = lax.dot_general(
        drive_low, skeleton_in, contract_panels, preferred_element_type=jnp.float32
    )
    gradient_part = lax.dot_general(
        loads_low, skeleton_out, contract_panels, preferred_element_type=jnp.float32
    )
    charges, gradient_all = lax.psum((charge_part, gradient_part), "rows")
    gradient = lax.dynamic_slice_in_dim(
        gradient_all, lax.axis_index("rows") * share_width, share_width, 1
    )

    def offsets_for(other_ids):
        offset = jnp.remainder(cluster - other_ids, clusters)
        active = (offset != 0).astype(jnp.float32)
        return (jnp.maximum(offset - 1, 0), active)

    charge_piece = lax.all_gather(charges[None], "blk", axis=0, tiled=True)
    span_count = charge_piece.shape[0]
    offset, active = offsets_for(jnp.arange(span_count, dtype=jnp.int32))
    chosen = jnp.take(kernels, offset, axis=0)
    potential = jnp.einsum(
        "cej,ckj->ek", charge_piece * active[:, None, None], chosen, precision=highest
    )
    potential_low = lax.all_gather(potential.astype(jnp.bfloat16), "rows", axis=1, tiled=True)
    far_ahead = jnp.dot(potential_low, skeleton_out, preferred_element_type=jnp.float32)
    offset, active = offsets_for(jnp.arange(lax.axis_size("blk") * 1, dtype=jnp.int32))
    chosen = jnp.take(kernels, offset, axis=0)
    summed = lax.psum_scatter(
        jnp.einsum("ek,ckj->cej", gradient, chosen, precision=highest) * active[:, None, None],
        "blk",
        scatter_dimension=0,
        tiled=True,
    )
    adjoint_low = lax.psum(summed[0], "rows").astype(jnp.bfloat16)
    far_behind = jnp.dot(adjoint_low, skeleton_in, preferred_element_type=jnp.float32)
    near_columns = lax.psum_scatter(
        near_behind.reshape(excite_count, column_blocks * tile_size),
        "rows",
        scatter_dimension=1,
        tiled=True,
    )
    response = near_ahead.reshape(excite_count, panels) + far_ahead
    sensitivity = near_columns + far_behind
    return (response, sensitivity)


MESH = pl.DeviceIdType.MESH
GROUP = 4
VMEM_BYTES = 62 * 1024 * 1024
bf16 = jnp.bfloat16
f32 = jnp.float32


def dot_nt(a, b):
    return lax.dot_general(a, b, (((1,), (1,)), ((), ())), preferred_element_type=f32)


def dot_nn(a, b):
    return jnp.dot(a, b, preferred_element_type=f32)


def kernel(
    rows,
    clusters,
    count_ref,
    tile_row_hbm,
    tile_col_hbm,
    drive_hbm,
    loads_hbm,
    tiles_hbm,
    skin_hbm,
    skout_hbm,
    trans_hbm,
    response_hbm,
    sensitivity_hbm,
    response_ref,
    sensitivity_ref,
    tile_row_ref,
    tile_col_ref,
    drive_ref,
    loads_ref,
    tiles,
    skin,
    skout,
    trans,
    trans_low,
    drive_all,
    loads_low,
    grad_part,
    grad_send,
    grad_recv,
    charge_part,
    charge_send,
    charge_recv,
    q_all,
    sib_send,
    sib_recv,
    plane_send,
    plane_recv,
    adj_part,
    adj_send,
    adj_recv,
    adj_all,
    pot_all,
    near_fwd,
    near_adj,
    near_send,
    near_first,
    near_pair,
    near_mid,
    near_back,
    near_last,
    local_sem,
    send_sem,
    grad_sem,
    charge_sem,
    drive_sem,
    qz_sem,
    qp_sem,
    qs_sem,
    sib_sem,
    plane_sem,
    adj_sem,
    adjall_sem,
    pot_sem,
    near_sem,
):
    chips = clusters // 2
    b = lax.axis_index("blk")
    r = lax.axis_index("rows")
    core = lax.rem(b, 2)
    chip = lax.div(b, 2)
    cap, size = tiles.shape[0], tiles.shape[1]
    share = q_all.shape[3]
    row_blocks = loads_low.shape[0]
    column_blocks = rows * row_blocks
    offsets = trans.shape[0]

    def row_at(step):
        return lax.rem(r + step + rows, rows)

    def blk_at(step, which):
        return lax.rem(chip + step + chips, chips) * 2 + which

    sibling = b + 1 - 2 * core

    local = []

    def fetch(src, dst):
        copy = pltpu.make_async_copy(src, dst, local_sem.at[len(local)])
        copy.start()
        local.append(copy)
        return copy

    get_loads = fetch(loads_hbm, loads_ref)
    get_out = fetch(skout_hbm, skout)
    get_drive = fetch(drive_hbm, drive_ref)
    get_in = fetch(skin_hbm, skin)
    get_trans = [fetch(trans_hbm.at[d], trans.at[d]) for d in range(offsets)]
    get_tiles = fetch(tiles_hbm, tiles)
    get_lists = [
        fetch(tile_row_hbm, tile_row_ref),
        fetch(tile_col_hbm, tile_col_ref),
    ]

    sent = []

    def send(src, dst, recv, blk, row, only=None):
        copy = pltpu.make_async_remote_copy(
            src_ref=src,
            dst_ref=dst,
            send_sem=send_sem.at[len(sent)],
            recv_sem=recv,
            device_id=(blk, row),
            device_id_type=MESH,
        )
        if only is None:
            copy.start()
        else:
            pl.when(only)(copy.start)
        sent.append((copy, only))
        return copy

    def send_later(src, dst, recv, blk, row):
        copy = pltpu.make_async_remote_copy(
            src_ref=src,
            dst_ref=dst,
            send_sem=send_sem.at[len(sent)],
            recv_sem=recv,
            device_id=(blk, row),
            device_id_type=MESH,
        )
        sent.append((copy, inner))
        return copy

    inner = lax.rem(r + 1, rows) >= 2
    outer = lax.rem(r + 1, rows) < 2
    mate = r + 1 - 2 * lax.rem(r, 2)
    opposite = rows - 1 - r
    pair = r - lax.rem(r, 2)
    far_pair = rows - 2 - pair

    def blocks_of(row, count):
        return pl.ds(row * row_blocks, count * row_blocks)

    barrier = pltpu.get_barrier_semaphore()
    partners = [(b, row_at(o)) for o in range(1, rows)]
    partners += [(blk_at(o, core), r) for o in range(1, chips)]
    partners += [(sibling, r)]
    for partner in partners:
        pl.semaphore_signal(barrier, inc=1, device_id=partner, device_id_type=MESH)

    get_loads.wait()
    for i in range(row_blocks):
        loads_low[i] = loads_ref[:, i * size : (i + 1) * size].astype(bf16)
    loads_wide = loads_ref[...].astype(bf16)
    get_out.wait()
    for j in range(rows):
        part = dot_nt(loads_wide, skout[j * share : (j + 1) * share, :])
        grad_part[j] = part
        grad_send[j] = part.astype(bf16)
    pl.semaphore_wait(barrier, len(partners))
    grad_copies = [
        send(grad_send.at[row_at(o)], grad_recv.at[o - 1], grad_sem.at[o - 1], b, row_at(o))
        for o in range(1, rows)
    ]
    get_drive.wait()
    for i in range(row_blocks):
        drive_all[r * row_blocks + i] = drive_ref[:, i * size : (i + 1) * size].astype(bf16)
    drive_wide = drive_ref[...].astype(bf16)
    get_in.wait()
    for j in range(rows):
        part = dot_nt(drive_wide, skin[j * share : (j + 1) * share, :])
        charge_part[j] = part
        charge_send[j] = part.astype(bf16)
    charge_copies = [
        send(charge_send.at[row_at(o)], charge_recv.at[o - 1], charge_sem.at[o - 1], b, row_at(o))
        for o in range(1, rows)
    ]

    for d in range(offsets):
        get_trans[d].wait()
        trans_low[d] = trans[d].astype(bf16)

    for copy in grad_copies:
        copy.wait_recv()
    gradient = grad_part[r]
    for o in range(rows - 1):
        gradient += grad_recv[o].astype(f32)
    grad_high = gradient.astype(bf16)
    grad_rest = (gradient - grad_high.astype(f32)).astype(bf16)
    grad_both = jnp.concatenate([grad_high, grad_rest], axis=0)
    excite = gradient.shape[0]

    def adjoint_term(target, j):
        index = lax.rem(b - target + clusters, clusters) - 1
        both = dot_nn(grad_both, trans_low[index, :, j * share : (j + 1) * share])
        return both[:excite] + both[excite:]

    sib_copies = []
    for o in range(chips):
        for j in range(rows):
            sib_send[o, j] = adjoint_term(blk_at(o, 1 - core), j).astype(bf16)
        sib_copies.append(send(sib_send.at[o], sib_recv.at[o], sib_sem.at[o], sibling, r))

    for copy in charge_copies:
        copy.wait_recv()
    charge = charge_part[r]
    for o in range(rows - 1):
        charge += charge_recv[o].astype(f32)
    q_all[r, b] = charge.astype(bf16)

    def send_quarter_to_plane(z):
        piece = q_all.at[row_at(-z), b]
        copies = [
            send(piece, piece, qp_sem.at[z, o - 1], blk_at(o, core), r) for o in range(1, chips)
        ]
        return copies, [send(piece, piece, qs_sem.at[z, 0], sibling, r)]

    piece = q_all.at[r, b]
    qz_copies = [send(piece, piece, qz_sem.at[o - 1], b, row_at(o)) for o in range(1, rows)]
    plane_q, sibling_q = [None] * rows, [None] * rows
    plane_q[0], sibling_q[0] = send_quarter_to_plane(0)

    piece = drive_all.at[blocks_of(r, 1)]
    drive_first = send(piece, piece, drive_sem.at[0], b, mate)

    plane_copies = []
    for o in range(1, chips):
        terms = [adjoint_term(blk_at(o, core), j) for j in range(rows)]
        sib_copies[o].wait_recv()
        for j in range(rows):
            plane_send[o - 1, j] = (terms[j] + sib_recv[o, j].astype(f32)).astype(bf16)
        plane_copies.append(
            send(
                plane_send.at[o - 1],
                plane_recv.at[o - 1],
                plane_sem.at[o - 1],
                blk_at(o, core),
                r,
            )
        )

    for z in range(1, rows):
        qz_copies[z - 1].wait_recv()
        plane_q[z], sibling_q[z] = send_quarter_to_plane(z)

    drive_first.wait_recv()
    piece = drive_all.at[blocks_of(pair, 2)]
    send(piece, piece, drive_sem.at[1], b, opposite, inner)

    near_adj[...] = jnp.zeros_like(near_adj)
    near_fwd[...] = jnp.zeros_like(near_fwd)
    get_tiles.wait()
    for copy in get_lists:
        copy.wait()

    used = count_ref[0]

    def adjoint_group(group, carry):
        products, columns = [], []
        for t in range(GROUP):
            slot = group * GROUP + t
            source = loads_low[tile_row_ref[slot]]
            products.append(dot_nn(source, tiles[slot]))
            columns.append(jnp.where(slot < used, tile_col_ref[slot], -1))
        for c in range(column_blocks):
            total = near_adj[c]
            for t in range(GROUP):
                total += products[t] * jnp.where(columns[t] == c, 1.0, 0.0).astype(f32)
            near_adj[c] = total
        return carry

    def forward_group(group, carry):
        products, targets = [], []
        for t in range(GROUP):
            slot = group * GROUP + t
            source = drive_all[tile_col_ref[slot]]
            products.append(dot_nt(source, tiles[slot]))
            targets.append(jnp.where(slot < used, tile_row_ref[slot], -1))
        for i in range(row_blocks):
            total = near_fwd[i]
            for t in range(GROUP):
                total += products[t] * jnp.where(targets[t] == i, 1.0, 0.0).astype(f32)
            near_fwd[i] = total
        return carry

    groups = cap // GROUP
    lax.fori_loop(0, groups, adjoint_group, 0)
    for c in range(column_blocks):
        near_send[c] = near_adj[c].astype(bf16)
    near_far = send(near_send.at[blocks_of(far_pair, 2)], near_pair, near_sem.at[1], b, mate, outer)
    near_mate = send(near_send.at[blocks_of(mate, 1)], near_first, near_sem.at[0], b, mate)
    piece = drive_all.at[blocks_of(far_pair, 2)]
    drive_last = send_later(piece, piece, drive_sem.at[1], b, mate)
    drive_last.wait_recv()
    pl.when(inner)(drive_last.start)

    sib_copies[0].wait_recv()
    for copy in plane_copies:
        copy.wait_recv()
    for j in range(rows):
        total = sib_recv[0, j].astype(f32)
        for o in range(chips - 1):
            total += plane_recv[o, j].astype(f32)
        adj_part[j] = total
        adj_send[j] = total.astype(bf16)
    adj_copies = [
        send(adj_send.at[row_at(o)], adj_recv.at[o - 1], adj_sem.at[o - 1], b, row_at(o))
        for o in range(1, rows)
    ]


    for z in range(rows):
        for o in range(1, chips):
            plane_q[z][o - 1].wait_recv()
            piece = q_all.at[row_at(-z), blk_at(-o, core)]
            sibling_q[z].append(send(piece, piece, qs_sem.at[z, o], sibling, r))

    @pl.when(inner)
    def _():
        near_far.wait_recv()
        for i in range(2 * row_blocks):
            total = near_adj[far_pair * row_blocks + i] + near_pair[i].astype(f32)
            near_mid[i] = total.astype(bf16)

    near_cross = send(near_mid, near_back, near_sem.at[2], b, opposite, inner)
    lax.fori_loop(0, groups // 2, forward_group, 0)

    for copy in adj_copies:
        copy.wait_recv()
    adjoint = adj_part[r]
    for o in range(rows - 1):
        adjoint += adj_recv[o].astype(f32)
    adj_all[r] = adjoint.astype(bf16)
    piece = adj_all.at[r]
    adjall_copies = [send(piece, piece, adjall_sem.at[o - 1], b, row_at(o)) for o in range(1, rows)]

    pl.when(inner)(near_cross.wait_recv)
    part = near_back.at[pl.ds((mate - pair) * row_blocks, row_blocks)]
    near_give = send(part, near_last, near_sem.at[3], b, mate, inner)

    for z in range(rows):
        for copy in sibling_q[z]:
            copy.wait_recv()
    potential = jnp.zeros((excite, share), f32)
    for j in range(rows):
        for d in range(1, offsets + 1):
            source = q_all[j, lax.rem(b - d + clusters, clusters)]
            potential += dot_nt(source, trans_low[d - 1, :, j * share : (j + 1) * share])
    pot_all[r] = potential.astype(bf16)
    piece = pot_all.at[r]
    pot_copies = [send(piece, piece, pot_sem.at[o - 1], b, row_at(o)) for o in range(1, rows)]

    lax.fori_loop(groups // 2, groups, forward_group, 0)

    near_mate.wait_recv()
    pl.when(outer)(near_give.wait_recv)

    @pl.when(inner)
    def _():
        for i in range(row_blocks):
            near_last[i] = near_back[(r - pair) * row_blocks + i]

    for i in range(row_blocks):
        total = near_adj[r * row_blocks + i] + near_first[i].astype(f32)
        near_adj[r * row_blocks + i] = total + near_last[i].astype(f32)

    for copy in pot_copies:
        copy.wait_recv()
    for i in range(row_blocks):
        total = near_fwd[i]
        for j in range(rows):
            block = skout[j * share : (j + 1) * share, i * size : (i + 1) * size]
            total += dot_nn(pot_all[j], block)
        response_ref[:, i * size : (i + 1) * size] = total
    put_response = fetch(response_ref, response_hbm)
    for copy in adjall_copies:
        copy.wait_recv()
    for i in range(row_blocks):
        total = near_adj[r * row_blocks + i]
        for j in range(rows):
            block = skin[j * share : (j + 1) * share, i * size : (i + 1) * size]
            total += dot_nn(adj_all[j], block)
        sensitivity_ref[:, i * size : (i + 1) * size] = total
    put_sensitivity = fetch(sensitivity_ref, sensitivity_hbm)
    for copy, only in sent:
        if only is None:
            copy.wait_send()
        else:
            pl.when(only)(copy.wait_send)
    put_response.wait()
    put_sensitivity.wait()


def landing(response, sensitivity, response_out, sensitivity_out):
    response_out[...] = response[...]
    sensitivity_out[...] = sensitivity[...]


def fused_plan(
    rows,
    clusters,
    excitations,
    adjoint_loads,
    near_tiles,
    tile_rows,
    tile_cols,
    tile_count,
    skeleton_in,
    skeleton_out,
    translation,
):
    kernels = translation[0]
    excite, panels = excitations.shape
    cap, size = near_tiles.shape[:2]
    offsets, share, points = kernels.shape
    chips = clusters // 2
    row_blocks = panels // size
    blocks = rows * row_blocks
    others = rows - 1
    sends = 6 * others + 3 + 4 + rows * (chips - 1) + rows * chips + chips + chips - 1
    vmem, dma = pltpu.VMEM, pltpu.SemaphoreType.DMA
    scratch = [
        vmem((excite, panels), f32),
        vmem((excite, panels), f32),
        pltpu.SMEM(tile_rows.shape, jnp.int32),
        pltpu.SMEM(tile_cols.shape, jnp.int32),
        vmem((excite, panels), f32),
        vmem((excite, panels), f32),
        vmem((cap, size, size), bf16),
        vmem((points, panels), bf16),
        vmem((points, panels), bf16),
        vmem((offsets, share, points), f32),
        vmem((offsets, share, points), bf16),
        vmem((blocks, excite, size), bf16),
        vmem((row_blocks, excite, size), bf16),
        vmem((rows, excite, share), f32),
        vmem((rows, excite, share), bf16),
        vmem((others, excite, share), bf16),
        vmem((rows, excite, share), f32),
        vmem((rows, excite, share), bf16),
        vmem((others, excite, share), bf16),
        vmem((rows, clusters, excite, share), bf16),
        vmem((chips, rows, excite, share), bf16),
        vmem((chips, rows, excite, share), bf16),
        vmem((chips - 1, rows, excite, share), bf16),
        vmem((chips - 1, rows, excite, share), bf16),
        vmem((rows, excite, share), f32),
        vmem((rows, excite, share), bf16),
        vmem((others, excite, share), bf16),
        vmem((rows, excite, share), bf16),
        vmem((rows, excite, share), bf16),
        vmem((row_blocks, excite, size), f32),
        vmem((blocks, excite, size), f32),
        vmem((blocks, excite, size), bf16),
        vmem((row_blocks, excite, size), bf16),
        vmem((2 * row_blocks, excite, size), bf16),
        vmem((2 * row_blocks, excite, size), bf16),
        vmem((2 * row_blocks, excite, size), bf16),
        vmem((row_blocks, excite, size), bf16),
        dma((offsets + 9,)),
        dma((sends,)),
        dma((others,)),
        dma((others,)),
        dma((2,)),
        dma((others,)),
        dma((rows, chips - 1)),
        dma((rows, chips)),
        dma((chips,)),
        dma((chips - 1,)),
        dma((others,)),
        dma((others,)),
        dma((others,)),
        dma((4,)),
    ]
    whole_vmem = pl.BlockSpec(memory_space=pltpu.VMEM)
    anywhere = pl.BlockSpec(memory_space=pl.ANY)
    results = pl.pallas_call(
        functools.partial(kernel, rows, clusters),
        out_shape=[jax.ShapeDtypeStruct((excite, panels), f32)] * 2,
        in_specs=[pl.BlockSpec(memory_space=pltpu.SMEM)] + [anywhere] * 8,
        out_specs=[anywhere] * 2,
        scratch_shapes=scratch,
        compiler_params=pltpu.CompilerParams(
            collective_id=0, has_side_effects=True, vmem_limit_bytes=VMEM_BYTES
        ),
    )(
        tile_count,
        tile_rows,
        tile_cols,
        excitations,
        adjoint_loads,
        near_tiles,
        skeleton_in,
        skeleton_out,
        kernels,
    )
    return pl.pallas_call(
        landing,
        out_shape=[jax.ShapeDtypeStruct((excite, panels), f32)] * 2,
        in_specs=[whole_vmem] * 2,
        out_specs=[whole_vmem] * 2,
        compiler_params=pltpu.CompilerParams(vmem_limit_bytes=VMEM_BYTES),
    )(*results)


def solution(mesh):
    clusters, rows = mesh.shape["blk"], mesh.shape["rows"]

    def on_device(*args):
        share = args[8].shape[2]
        tile_size = args[2].shape[1]
        fits = clusters == 8 and rows == 4 and share % 128 == 0
        if fits and tile_size % 128 == 0 and args[2].shape[0] % (2 * GROUP) == 0:
            return tuple(fused_plan(rows, clusters, *args))
        return plain_plan(*args)

    return jax.shard_map(
        on_device,
        mesh=mesh,
        in_specs=(
            P(None, ("blk", "rows")),
            P(None, ("blk", "rows")),
            P(("blk", "rows"), None, None),
            P(("blk", "rows")),
            P(("blk", "rows")),
            P(("blk", "rows")),
            P(None, ("blk", "rows")),
            P(None, ("blk", "rows")),
            P("blk", None, "rows", None),
        ),
        out_specs=(P(None, ("blk", "rows")), P(None, ("blk", "rows"))),
        check_vma=False,
    )
```

```python
import functools

import jax
import jax.numpy as jnp
from jax import lax
from jax.experimental import pallas as pl
from jax.experimental.pallas import tpu as pltpu
from jax.sharding import PartitionSpec as P

highest = lax.Precision.HIGHEST


def plain_plan(
    excitations,
    adjoint_loads,
    near_tiles,
    tile_rows,
    tile_cols,
    tile_count,
    skeleton_in,
    skeleton_out,
    translation,
):
    drive_low = excitations.astype(jnp.bfloat16)
    loads_low = adjoint_loads.astype(jnp.bfloat16)
    excite_count = excitations.shape[0]
    panels = excitations.shape[1]
    tile_size = near_tiles.shape[1]
    kernels = translation[0]
    share_width = kernels.shape[1]
    clusters = lax.axis_size("blk")
    cluster = lax.axis_index("blk")
    gathered = lax.all_gather(drive_low, "rows", axis=1, tiled=True)
    column_blocks = gathered.shape[1] // tile_size
    row_blocks = panels // tile_size
    drive_blocks = gathered.reshape(excite_count, column_blocks, tile_size)
    load_blocks = loads_low.reshape(excite_count, row_blocks, tile_size)
    used_slots = tile_count[0]

    def near_group(group_index, carry):
        ahead, behind = carry
        first_slot = group_index * 4
        tile_group = lax.dynamic_slice_in_dim(near_tiles, first_slot, 4, 0)
        row_ids = lax.dynamic_slice_in_dim(tile_rows, first_slot, 4, 0)
        column_ids = lax.dynamic_slice_in_dim(tile_cols, first_slot, 4, 0)
        live_mask = (first_slot + jnp.arange(4, dtype=jnp.int32) < used_slots).astype(jnp.float32)[
            None, :, None
        ]
        source = jnp.take(drive_blocks, column_ids, axis=1)
        target = jnp.take(load_blocks, row_ids, axis=1)
        forward = (
            jnp.einsum("egj,gij->egi", source, tile_group, preferred_element_type=jnp.float32)
            * live_mask
        )
        backward = (
            jnp.einsum("egi,gij->egj", target, tile_group, preferred_element_type=jnp.float32)
            * live_mask
        )
        return (ahead.at[:, row_ids].add(forward), behind.at[:, column_ids].add(backward))

    near_start = (
        jnp.zeros((excite_count, row_blocks, tile_size), jnp.float32),
        jnp.zeros((excite_count, column_blocks, tile_size), jnp.float32),
    )
    near_ahead, near_behind = lax.fori_loop(0, (used_slots + 3) // 4, near_group, near_start)
    contract_panels = (((1,), (1,)), ((), ()))
    charge_part = lax.dot_general(
        drive_low, skeleton_in, contract_panels, preferred_element_type=jnp.float32
    )
    gradient_part = lax.dot_general(
        loads_low, skeleton_out, contract_panels, preferred_element_type=jnp.float32
    )
    charges, gradient_all = lax.psum((charge_part, gradient_part), "rows")
    gradient = lax.dynamic_slice_in_dim(
        gradient_all, lax.axis_index("rows") * share_width, share_width, 1
    )

    def offsets_for(other_ids):
        offset = jnp.remainder(cluster - other_ids, clusters)
        active = (offset != 0).astype(jnp.float32)
        return (jnp.maximum(offset - 1, 0), active)

    charge_piece = lax.all_gather(charges[None], "blk", axis=0, tiled=True)
    span_count = charge_piece.shape[0]
    offset, active = offsets_for(jnp.arange(span_count, dtype=jnp.int32))
    chosen = jnp.take(kernels, offset, axis=0)
    potential = jnp.einsum(
        "cej,ckj->ek", charge_piece * active[:, None, None], chosen, precision=highest
    )
    potential_low = lax.all_gather(potential.astype(jnp.bfloat16), "rows", axis=1, tiled=True)
    far_ahead = jnp.dot(potential_low, skeleton_out, preferred_element_type=jnp.float32)
    offset, active = offsets_for(jnp.arange(lax.axis_size("blk") * 1, dtype=jnp.int32))
    chosen = jnp.take(kernels, offset, axis=0)
    summed = lax.psum_scatter(
        jnp.einsum("ek,ckj->cej", gradient, chosen, precision=highest) * active[:, None, None],
        "blk",
        scatter_dimension=0,
        tiled=True,
    )
    adjoint_low = lax.psum(summed[0], "rows").astype(jnp.bfloat16)
    far_behind = jnp.dot(adjoint_low, skeleton_in, preferred_element_type=jnp.float32)
    near_columns = lax.psum_scatter(
        near_behind.reshape(excite_count, column_blocks * tile_size),
        "rows",
        scatter_dimension=1,
        tiled=True,
    )
    response = near_ahead.reshape(excite_count, panels) + far_ahead
    sensitivity = near_columns + far_behind
    return (response, sensitivity)


MESH = pl.DeviceIdType.MESH
GROUP = 4
VMEM_BYTES = 62 * 1024 * 1024
bf16 = jnp.bfloat16
f32 = jnp.float32


def dot_nt(a, b):
    return lax.dot_general(a, b, (((1,), (1,)), ((), ())), preferred_element_type=f32)


def dot_nn(a, b):
    return jnp.dot(a, b, preferred_element_type=f32)


def kernel(
    rows,
    clusters,
    count_ref,
    tile_row_hbm,
    tile_col_hbm,
    drive_hbm,
    loads_hbm,
    tiles_hbm,
    skin_hbm,
    skout_hbm,
    trans_hbm,
    response_hbm,
    sensitivity_hbm,
    response_ref,
    sensitivity_ref,
    tile_row_ref,
    tile_col_ref,
    drive_ref,
    loads_ref,
    tiles,
    skin,
    skout,
    trans,
    trans_low,
    drive_all,
    loads_low,
    grad_part,
    grad_send,
    grad_recv,
    charge_part,
    charge_send,
    charge_recv,
    q_all,
    sib_send,
    sib_recv,
    plane_send,
    plane_recv,
    adj_part,
    adj_send,
    adj_recv,
    adj_all,
    pot_all,
    near_fwd,
    near_adj,
    near_send,
    near_recv,
    local_sem,
    send_sem,
    grad_sem,
    charge_sem,
    drive_sem,
    qz_sem,
    qp_sem,
    qs_sem,
    sib_sem,
    plane_sem,
    adj_sem,
    adjall_sem,
    pot_sem,
    near_sem,
):
    chips = clusters // 2
    b = lax.axis_index("blk")
    r = lax.axis_index("rows")
    core = lax.rem(b, 2)
    chip = lax.div(b, 2)
    cap, size = tiles.shape[0], tiles.shape[1]
    share = q_all.shape[3]
    row_blocks = loads_low.shape[0]
    column_blocks = rows * row_blocks
    offsets = trans.shape[0]

    def row_at(step):
        return lax.rem(r + step + rows, rows)

    def blk_at(step, which):
        return lax.rem(chip + step + chips, chips) * 2 + which

    sibling = b + 1 - 2 * core

    local = []

    def fetch(src, dst):
        copy = pltpu.make_async_copy(src, dst, local_sem.at[len(local)])
        copy.start()
        local.append(copy)
        return copy

    get_loads = fetch(loads_hbm, loads_ref)
    get_out = fetch(skout_hbm, skout)
    get_drive = fetch(drive_hbm, drive_ref)
    get_in = fetch(skin_hbm, skin)
    get_trans = [fetch(trans_hbm.at[d], trans.at[d]) for d in range(offsets)]
    get_tiles = fetch(tiles_hbm, tiles)
    get_lists = [
        fetch(tile_row_hbm, tile_row_ref),
        fetch(tile_col_hbm, tile_col_ref),
    ]

    sent = []

    def send(src, dst, recv, blk, row):
        copy = pltpu.make_async_remote_copy(
            src_ref=src,
            dst_ref=dst,
            send_sem=send_sem.at[len(sent)],
            recv_sem=recv,
            device_id=(blk, row),
            device_id_type=MESH,
        )
        copy.start()
        sent.append(copy)
        return copy

    barrier = pltpu.get_barrier_semaphore()
    partners = [(b, row_at(o)) for o in range(1, rows)]
    partners += [(blk_at(o, core), r) for o in range(1, chips)]
    partners += [(sibling, r)]
    for partner in partners:
        pl.semaphore_signal(barrier, inc=1, device_id=partner, device_id_type=MESH)

    get_loads.wait()
    for i in range(row_blocks):
        loads_low[i] = loads_ref[:, i * size : (i + 1) * size].astype(bf16)
    loads_wide = loads_ref[...].astype(bf16)
    get_out.wait()
    for j in range(rows):
        part = dot_nt(loads_wide, skout[j * share : (j + 1) * share, :])
        grad_part[j] = part
        grad_send[j] = part.astype(bf16)
    pl.semaphore_wait(barrier, len(partners))
    grad_copies = [
        send(grad_send.at[row_at(o)], grad_recv.at[o - 1], grad_sem.at[o - 1], b, row_at(o))
        for o in range(1, rows)
    ]
    get_drive.wait()
    for i in range(row_blocks):
        drive_all[r * row_blocks + i] = drive_ref[:, i * size : (i + 1) * size].astype(bf16)
    drive_wide = drive_ref[...].astype(bf16)
    get_in.wait()
    for j in range(rows):
        part = dot_nt(drive_wide, skin[j * share : (j + 1) * share, :])
        charge_part[j] = part
        charge_send[j] = part.astype(bf16)
    charge_copies = [
        send(charge_send.at[row_at(o)], charge_recv.at[o - 1], charge_sem.at[o - 1], b, row_at(o))
        for o in range(1, rows)
    ]

    for d in range(offsets):
        get_trans[d].wait()
        trans_low[d] = trans[d].astype(bf16)

    for copy in grad_copies:
        copy.wait_recv()
    gradient = grad_part[r]
    for o in range(rows - 1):
        gradient += grad_recv[o].astype(f32)
    grad_high = gradient.astype(bf16)
    grad_rest = (gradient - grad_high.astype(f32)).astype(bf16)
    grad_both = jnp.concatenate([grad_high, grad_rest], axis=0)
    excite = gradient.shape[0]

    def adjoint_term(target, j):
        index = lax.rem(b - target + clusters, clusters) - 1
        both = dot_nn(grad_both, trans_low[index, :, j * share : (j + 1) * share])
        return both[:excite] + both[excite:]

    sib_copies = []
    for o in range(chips):
        for j in range(rows):
            sib_send[o, j] = adjoint_term(blk_at(o, 1 - core), j).astype(bf16)
        sib_copies.append(send(sib_send.at[o], sib_recv.at[o], sib_sem.at[o], sibling, r))

    for copy in charge_copies:
        copy.wait_recv()
    charge = charge_part[r]
    for o in range(rows - 1):
        charge += charge_recv[o].astype(f32)
    q_all[b, r] = charge.astype(bf16)

    piece = q_all.at[b, r]
    qz_copies = [send(piece, piece, qz_sem.at[o - 1], b, row_at(o)) for o in range(1, rows)]

    mine = pl.ds(r * row_blocks, row_blocks)
    drive_copies = [
        send(drive_all.at[mine], drive_all.at[mine], drive_sem.at[o - 1], b, row_at(o))
        for o in range(1, rows)
    ]

    plane_copies = []
    for o in range(1, chips):
        terms = [adjoint_term(blk_at(o, core), j) for j in range(rows)]
        sib_copies[o].wait_recv()
        for j in range(rows):
            plane_send[o - 1, j] = (terms[j] + sib_recv[o, j].astype(f32)).astype(bf16)
        plane_copies.append(
            send(
                plane_send.at[o - 1],
                plane_recv.at[o - 1],
                plane_sem.at[o - 1],
                blk_at(o, core),
                r,
            )
        )

    for copy in qz_copies:
        copy.wait_recv()
    piece = q_all.at[b]
    plane_q = [send(piece, piece, qp_sem.at[o - 1], blk_at(o, core), r) for o in range(1, chips)]
    sibling_q = [send(piece, piece, qs_sem.at[0], sibling, r)]

    near_adj[...] = jnp.zeros_like(near_adj)
    near_fwd[...] = jnp.zeros_like(near_fwd)
    get_tiles.wait()
    for copy in get_lists:
        copy.wait()

    used = count_ref[0]

    def adjoint_group(group, carry):
        products, columns = [], []
        for t in range(GROUP):
            slot = group * GROUP + t
            source = loads_low[tile_row_ref[slot]]
            products.append(dot_nn(source, tiles[slot]))
            columns.append(jnp.where(slot < used, tile_col_ref[slot], -1))
        for c in range(column_blocks):
            total = near_adj[c]
            for t in range(GROUP):
                total += products[t] * jnp.where(columns[t] == c, 1.0, 0.0).astype(f32)
            near_adj[c] = total
        return carry

    def forward_group(group, carry):
        products, targets = [], []
        for t in range(GROUP):
            slot = group * GROUP + t
            source = drive_all[tile_col_ref[slot]]
            products.append(dot_nt(source, tiles[slot]))
            targets.append(jnp.where(slot < used, tile_row_ref[slot], -1))
        for i in range(row_blocks):
            total = near_fwd[i]
            for t in range(GROUP):
                total += products[t] * jnp.where(targets[t] == i, 1.0, 0.0).astype(f32)
            near_fwd[i] = total
        return carry

    groups = cap // GROUP
    lax.fori_loop(0, groups, adjoint_group, 0)
    sib_copies[0].wait_recv()
    for copy in plane_copies:
        copy.wait_recv()
    for j in range(rows):
        total = sib_recv[0, j].astype(f32)
        for o in range(chips - 1):
            total += plane_recv[o, j].astype(f32)
        adj_part[j] = total
        adj_send[j] = total.astype(bf16)
    adj_copies = [
        send(adj_send.at[row_at(o)], adj_recv.at[o - 1], adj_sem.at[o - 1], b, row_at(o))
        for o in range(1, rows)
    ]

    for c in range(column_blocks):
        near_send[c] = near_adj[c].astype(bf16)
    near_copies = [
        send(
            near_send.at[pl.ds(row_at(o) * row_blocks, row_blocks)],
            near_recv.at[o - 1],
            near_sem.at[o - 1],
            b,
            row_at(o),
        )
        for o in range(1, rows)
    ]

    for o in range(1, chips):
        plane_q[o - 1].wait_recv()
        piece = q_all.at[blk_at(-o, core)]
        sibling_q.append(send(piece, piece, qs_sem.at[o], sibling, r))

    for copy in drive_copies:
        copy.wait_recv()
    lax.fori_loop(0, groups // 2, forward_group, 0)

    for copy in adj_copies:
        copy.wait_recv()
    adjoint = adj_part[r]
    for o in range(rows - 1):
        adjoint += adj_recv[o].astype(f32)
    adj_all[r] = adjoint.astype(bf16)
    piece = adj_all.at[r]
    adjall_copies = [send(piece, piece, adjall_sem.at[o - 1], b, row_at(o)) for o in range(1, rows)]

    for copy in sibling_q:
        copy.wait_recv()
    potential = jnp.zeros((excite, share), f32)
    for j in range(rows):
        for d in range(1, offsets + 1):
            source = q_all[lax.rem(b - d + clusters, clusters), j]
            potential += dot_nt(source, trans_low[d - 1, :, j * share : (j + 1) * share])
    pot_all[r] = potential.astype(bf16)
    piece = pot_all.at[r]
    pot_copies = [send(piece, piece, pot_sem.at[o - 1], b, row_at(o)) for o in range(1, rows)]

    lax.fori_loop(groups // 2, groups, forward_group, 0)

    for copy in near_copies:
        copy.wait_recv()
    for i in range(row_blocks):
        total = near_adj[r * row_blocks + i]
        for o in range(rows - 1):
            total += near_recv[o, i].astype(f32)
        near_adj[r * row_blocks + i] = total

    for copy in pot_copies:
        copy.wait_recv()
    for i in range(row_blocks):
        total = near_fwd[i]
        for j in range(rows):
            block = skout[j * share : (j + 1) * share, i * size : (i + 1) * size]
            total += dot_nn(pot_all[j], block)
        response_ref[:, i * size : (i + 1) * size] = total
    put_response = fetch(response_ref, response_hbm)
    for copy in adjall_copies:
        copy.wait_recv()
    for i in range(row_blocks):
        total = near_adj[r * row_blocks + i]
        for j in range(rows):
            block = skin[j * share : (j + 1) * share, i * size : (i + 1) * size]
            total += dot_nn(adj_all[j], block)
        sensitivity_ref[:, i * size : (i + 1) * size] = total
    put_sensitivity = fetch(sensitivity_ref, sensitivity_hbm)
    for copy in sent:
        copy.wait_send()
    put_response.wait()
    put_sensitivity.wait()


def landing(response, sensitivity, response_out, sensitivity_out):
    response_out[...] = response[...]
    sensitivity_out[...] = sensitivity[...]


def fused_plan(
    rows,
    clusters,
    excitations,
    adjoint_loads,
    near_tiles,
    tile_rows,
    tile_cols,
    tile_count,
    skeleton_in,
    skeleton_out,
    translation,
):
    kernels = translation[0]
    excite, panels = excitations.shape
    cap, size = near_tiles.shape[:2]
    offsets, share, points = kernels.shape
    chips = clusters // 2
    row_blocks = panels // size
    blocks = rows * row_blocks
    others = rows - 1
    sends = 7 * others + 3 * chips - 1 + chips - 1 + others
    vmem, dma = pltpu.VMEM, pltpu.SemaphoreType.DMA
    scratch = [
        vmem((excite, panels), f32),
        vmem((excite, panels), f32),
        pltpu.SMEM(tile_rows.shape, jnp.int32),
        pltpu.SMEM(tile_cols.shape, jnp.int32),
        vmem((excite, panels), f32),
        vmem((excite, panels), f32),
        vmem((cap, size, size), bf16),
        vmem((points, panels), bf16),
        vmem((points, panels), bf16),
        vmem((offsets, share, points), f32),
        vmem((offsets, share, points), bf16),
        vmem((blocks, excite, size), bf16),
        vmem((row_blocks, excite, size), bf16),
        vmem((rows, excite, share), f32),
        vmem((rows, excite, share), bf16),
        vmem((others, excite, share), bf16),
        vmem((rows, excite, share), f32),
        vmem((rows, excite, share), bf16),
        vmem((others, excite, share), bf16),
        vmem((clusters, rows, excite, share), bf16),
        vmem((chips, rows, excite, share), bf16),
        vmem((chips, rows, excite, share), bf16),
        vmem((chips - 1, rows, excite, share), bf16),
        vmem((chips - 1, rows, excite, share), bf16),
        vmem((rows, excite, share), f32),
        vmem((rows, excite, share), bf16),
        vmem((others, excite, share), bf16),
        vmem((rows, excite, share), bf16),
        vmem((rows, excite, share), bf16),
        vmem((row_blocks, excite, size), f32),
        vmem((blocks, excite, size), f32),
        vmem((blocks, excite, size), bf16),
        vmem((others, row_blocks, excite, size), bf16),
        dma((offsets + 9,)),
        dma((sends,)),
        dma((others,)),
        dma((others,)),
        dma((others,)),
        dma((others,)),
        dma((chips - 1,)),
        dma((chips,)),
        dma((chips,)),
        dma((chips - 1,)),
        dma((others,)),
        dma((others,)),
        dma((others,)),
        dma((others,)),
    ]
    whole_vmem = pl.BlockSpec(memory_space=pltpu.VMEM)
    anywhere = pl.BlockSpec(memory_space=pl.ANY)
    results = pl.pallas_call(
        functools.partial(kernel, rows, clusters),
        out_shape=[jax.ShapeDtypeStruct((excite, panels), f32)] * 2,
        in_specs=[pl.BlockSpec(memory_space=pltpu.SMEM)] + [anywhere] * 8,
        out_specs=[anywhere] * 2,
        scratch_shapes=scratch,
        compiler_params=pltpu.CompilerParams(
            collective_id=0, has_side_effects=True, vmem_limit_bytes=VMEM_BYTES
        ),
    )(
        tile_count,
        tile_rows,
        tile_cols,
        excitations,
        adjoint_loads,
        near_tiles,
        skeleton_in,
        skeleton_out,
        kernels,
    )
    return pl.pallas_call(
        landing,
        out_shape=[jax.ShapeDtypeStruct((excite, panels), f32)] * 2,
        in_specs=[whole_vmem] * 2,
        out_specs=[whole_vmem] * 2,
        compiler_params=pltpu.CompilerParams(vmem_limit_bytes=VMEM_BYTES),
    )(*results)


def solution(mesh):
    clusters, rows = mesh.shape["blk"], mesh.shape["rows"]

    def on_device(*args):
        share = args[8].shape[2]
        tile_size = args[2].shape[1]
        fits = clusters == 8 and rows == 4 and share % 128 == 0
        if fits and tile_size % 128 == 0 and args[2].shape[0] % (2 * GROUP) == 0:
            return tuple(fused_plan(rows, clusters, *args))
        return plain_plan(*args)

    return jax.shard_map(
        on_device,
        mesh=mesh,
        in_specs=(
            P(None, ("blk", "rows")),
            P(None, ("blk", "rows")),
            P(("blk", "rows"), None, None),
            P(("blk", "rows")),
            P(("blk", "rows")),
            P(("blk", "rows")),
            P(None, ("blk", "rows")),
            P(None, ("blk", "rows")),
            P("blk", None, "rows", None),
        ),
        out_specs=(P(None, ("blk", "rows")), P(None, ("blk", "rows"))),
        check_vma=False,
    )
```

```python
import functools

import jax
import jax.numpy as jnp
from jax import lax
from jax.experimental import pallas as pl
from jax.experimental.pallas import tpu as pltpu
from jax.sharding import PartitionSpec as P

highest = lax.Precision.HIGHEST


def plain_plan(
    excitations,
    adjoint_loads,
    near_tiles,
    tile_rows,
    tile_cols,
    tile_count,
    skeleton_in,
    skeleton_out,
    translation,
):
    drive_low = excitations.astype(jnp.bfloat16)
    loads_low = adjoint_loads.astype(jnp.bfloat16)
    excite_count = excitations.shape[0]
    panels = excitations.shape[1]
    tile_size = near_tiles.shape[1]
    kernels = translation[0]
    share_width = kernels.shape[1]
    clusters = lax.axis_size("blk")
    cluster = lax.axis_index("blk")
    gathered = lax.all_gather(drive_low, "rows", axis=1, tiled=True)
    column_blocks = gathered.shape[1] // tile_size
    row_blocks = panels // tile_size
    drive_blocks = gathered.reshape(excite_count, column_blocks, tile_size)
    load_blocks = loads_low.reshape(excite_count, row_blocks, tile_size)
    used_slots = tile_count[0]

    def near_group(group_index, carry):
        ahead, behind = carry
        first_slot = group_index * 4
        tile_group = lax.dynamic_slice_in_dim(near_tiles, first_slot, 4, 0)
        row_ids = lax.dynamic_slice_in_dim(tile_rows, first_slot, 4, 0)
        column_ids = lax.dynamic_slice_in_dim(tile_cols, first_slot, 4, 0)
        live_mask = (first_slot + jnp.arange(4, dtype=jnp.int32) < used_slots).astype(jnp.float32)[
            None, :, None
        ]
        source = jnp.take(drive_blocks, column_ids, axis=1)
        target = jnp.take(load_blocks, row_ids, axis=1)
        forward = (
            jnp.einsum("egj,gij->egi", source, tile_group, preferred_element_type=jnp.float32)
            * live_mask
        )
        backward = (
            jnp.einsum("egi,gij->egj", target, tile_group, preferred_element_type=jnp.float32)
            * live_mask
        )
        return (ahead.at[:, row_ids].add(forward), behind.at[:, column_ids].add(backward))

    near_start = (
        jnp.zeros((excite_count, row_blocks, tile_size), jnp.float32),
        jnp.zeros((excite_count, column_blocks, tile_size), jnp.float32),
    )
    near_ahead, near_behind = lax.fori_loop(0, (used_slots + 3) // 4, near_group, near_start)
    contract_panels = (((1,), (1,)), ((), ()))
    charge_part = lax.dot_general(
        drive_low, skeleton_in, contract_panels, preferred_element_type=jnp.float32
    )
    gradient_part = lax.dot_general(
        loads_low, skeleton_out, contract_panels, preferred_element_type=jnp.float32
    )
    charges, gradient_all = lax.psum((charge_part, gradient_part), "rows")
    gradient = lax.dynamic_slice_in_dim(
        gradient_all, lax.axis_index("rows") * share_width, share_width, 1
    )

    def offsets_for(other_ids):
        offset = jnp.remainder(cluster - other_ids, clusters)
        active = (offset != 0).astype(jnp.float32)
        return (jnp.maximum(offset - 1, 0), active)

    charge_piece = lax.all_gather(charges[None], "blk", axis=0, tiled=True)
    span_count = charge_piece.shape[0]
    offset, active = offsets_for(jnp.arange(span_count, dtype=jnp.int32))
    chosen = jnp.take(kernels, offset, axis=0)
    potential = jnp.einsum(
        "cej,ckj->ek", charge_piece * active[:, None, None], chosen, precision=highest
    )
    potential_low = lax.all_gather(potential.astype(jnp.bfloat16), "rows", axis=1, tiled=True)
    far_ahead = jnp.dot(potential_low, skeleton_out, preferred_element_type=jnp.float32)
    offset, active = offsets_for(jnp.arange(lax.axis_size("blk") * 1, dtype=jnp.int32))
    chosen = jnp.take(kernels, offset, axis=0)
    summed = lax.psum_scatter(
        jnp.einsum("ek,ckj->cej", gradient, chosen, precision=highest) * active[:, None, None],
        "blk",
        scatter_dimension=0,
        tiled=True,
    )
    adjoint_low = lax.psum(summed[0], "rows").astype(jnp.bfloat16)
    far_behind = jnp.dot(adjoint_low, skeleton_in, preferred_element_type=jnp.float32)
    near_columns = lax.psum_scatter(
        near_behind.reshape(excite_count, column_blocks * tile_size),
        "rows",
        scatter_dimension=1,
        tiled=True,
    )
    response = near_ahead.reshape(excite_count, panels) + far_ahead
    sensitivity = near_columns + far_behind
    return (response, sensitivity)


MESH = pl.DeviceIdType.MESH
GROUP = 4
VMEM_BYTES = 62 * 1024 * 1024
bf16 = jnp.bfloat16
f32 = jnp.float32


def dot_nt(a, b):
    return lax.dot_general(a, b, (((1,), (1,)), ((), ())), preferred_element_type=f32)


def dot_nn(a, b):
    return jnp.dot(a, b, preferred_element_type=f32)


def kernel(
    rows,
    clusters,
    count_ref,
    tile_row_hbm,
    tile_col_hbm,
    drive_hbm,
    loads_hbm,
    tiles_hbm,
    skin_hbm,
    skout_hbm,
    trans_hbm,
    response_hbm,
    sensitivity_hbm,
    response_ref,
    sensitivity_ref,
    tile_row_ref,
    tile_col_ref,
    drive_ref,
    loads_ref,
    tiles,
    skin,
    skout,
    trans,
    trans_low,
    drive_all,
    loads_low,
    grad_part,
    grad_send,
    grad_recv,
    charge_part,
    charge_send,
    charge_recv,
    q_all,
    sib_send,
    sib_recv,
    plane_send,
    plane_recv,
    adj_part,
    adj_send,
    adj_recv,
    adj_all,
    pot_all,
    near_fwd,
    near_adj,
    near_send,
    near_recv,
    local_sem,
    send_sem,
    grad_sem,
    charge_sem,
    drive_sem,
    qz_sem,
    qp_sem,
    qs_sem,
    sib_sem,
    plane_sem,
    adj_sem,
    adjall_sem,
    pot_sem,
    near_sem,
):
    chips = clusters // 2
    b = lax.axis_index("blk")
    r = lax.axis_index("rows")
    core = lax.rem(b, 2)
    chip = lax.div(b, 2)
    cap, size = tiles.shape[0], tiles.shape[1]
    share = q_all.shape[3]
    row_blocks = loads_low.shape[0]
    column_blocks = rows * row_blocks
    offsets = trans.shape[0]

    def row_at(step):
        return lax.rem(r + step + rows, rows)

    def blk_at(step, which):
        return lax.rem(chip + step + chips, chips) * 2 + which

    sibling = b + 1 - 2 * core

    local = []

    def fetch(src, dst):
        copy = pltpu.make_async_copy(src, dst, local_sem.at[len(local)])
        copy.start()
        local.append(copy)
        return copy

    get_loads = fetch(loads_hbm, loads_ref)
    get_out = fetch(skout_hbm, skout)
    get_drive = fetch(drive_hbm, drive_ref)
    get_in = fetch(skin_hbm, skin)
    get_trans = [fetch(trans_hbm.at[d], trans.at[d]) for d in range(offsets)]
    get_tiles = fetch(tiles_hbm, tiles)
    get_lists = [
        fetch(tile_row_hbm, tile_row_ref),
        fetch(tile_col_hbm, tile_col_ref),
    ]

    sent = []

    def send(src, dst, recv, blk, row):
        copy = pltpu.make_async_remote_copy(
            src_ref=src,
            dst_ref=dst,
            send_sem=send_sem.at[len(sent)],
            recv_sem=recv,
            device_id=(blk, row),
            device_id_type=MESH,
        )
        copy.start()
        sent.append(copy)
        return copy

    barrier = pltpu.get_barrier_semaphore()
    partners = [(b, row_at(o)) for o in range(1, rows)]
    partners += [(blk_at(o, core), r) for o in range(1, chips)]
    partners += [(sibling, r)]
    for partner in partners:
        pl.semaphore_signal(barrier, inc=1, device_id=partner, device_id_type=MESH)

    get_loads.wait()
    for i in range(row_blocks):
        loads_low[i] = loads_ref[:, i * size : (i + 1) * size].astype(bf16)
    loads_wide = loads_ref[...].astype(bf16)
    get_out.wait()
    for j in range(rows):
        part = dot_nt(loads_wide, skout[j * share : (j + 1) * share, :])
        grad_part[j] = part
        grad_send[j] = part.astype(bf16)
    pl.semaphore_wait(barrier, len(partners))
    grad_copies = [
        send(grad_send.at[row_at(o)], grad_recv.at[o - 1], grad_sem.at[o - 1], b, row_at(o))
        for o in range(1, rows)
    ]
    get_drive.wait()
    for i in range(row_blocks):
        drive_all[r * row_blocks + i] = drive_ref[:, i * size : (i + 1) * size].astype(bf16)
    drive_wide = drive_ref[...].astype(bf16)
    get_in.wait()
    for j in range(rows):
        part = dot_nt(drive_wide, skin[j * share : (j + 1) * share, :])
        charge_part[j] = part
        charge_send[j] = part.astype(bf16)
    charge_copies = [
        send(charge_send.at[row_at(o)], charge_recv.at[o - 1], charge_sem.at[o - 1], b, row_at(o))
        for o in range(1, rows)
    ]

    for d in range(offsets):
        get_trans[d].wait()
        trans_low[d] = trans[d].astype(bf16)

    for copy in grad_copies:
        copy.wait_recv()
    gradient = grad_part[r]
    for o in range(rows - 1):
        gradient += grad_recv[o].astype(f32)
    grad_high = gradient.astype(bf16)
    grad_rest = (gradient - grad_high.astype(f32)).astype(bf16)
    grad_both = jnp.concatenate([grad_high, grad_rest], axis=0)
    excite = gradient.shape[0]

    def adjoint_term(target, j):
        index = lax.rem(b - target + clusters, clusters) - 1
        both = dot_nn(grad_both, trans_low[index, :, j * share : (j + 1) * share])
        return both[:excite] + both[excite:]

    sib_copies = [None] * chips
    for o in [*range(1, chips), 0]:
        for j in range(rows):
            sib_send[o, j] = adjoint_term(blk_at(o, 1 - core), j).astype(bf16)
        sib_copies[o] = send(sib_send.at[o], sib_recv.at[o], sib_sem.at[o], sibling, r)

    for copy in charge_copies:
        copy.wait_recv()
    charge = charge_part[r]
    for o in range(rows - 1):
        charge += charge_recv[o].astype(f32)
    q_all[b, 0] = charge.astype(bf16)
    piece = q_all.at[b, 0]
    qz_copies = [
        send(piece, q_all.at[b, o], qz_sem.at[o - 1], b, row_at(o)) for o in range(1, rows)
    ]
    plane_q = [send(piece, piece, qp_sem.at[0, o - 1], blk_at(o, core), r) for o in range(1, chips)]

    mine = pl.ds(r * row_blocks, row_blocks)
    drive_copies = [
        send(drive_all.at[mine], drive_all.at[mine], drive_sem.at[o - 1], b, row_at(o))
        for o in range(1, rows)
    ]

    plane_copies = []
    for o in range(1, chips):
        terms = [adjoint_term(blk_at(o, core), j) for j in range(rows)]
        sib_copies[o].wait_recv()
        for j in range(rows):
            plane_send[o - 1, j] = (terms[j] + sib_recv[o, j].astype(f32)).astype(bf16)
        plane_copies.append(
            send(
                plane_send.at[o - 1],
                plane_recv.at[o - 1],
                plane_sem.at[o - 1],
                blk_at(o, core),
                r,
            )
        )

    near_adj[...] = jnp.zeros_like(near_adj)
    near_fwd[...] = jnp.zeros_like(near_fwd)
    get_tiles.wait()
    for copy in get_lists:
        copy.wait()

    used = count_ref[0]

    def adjoint_group(group, carry):
        products, columns = [], []
        for t in range(GROUP):
            slot = group * GROUP + t
            source = loads_low[tile_row_ref[slot]]
            products.append(dot_nn(source, tiles[slot]))
            columns.append(jnp.where(slot < used, tile_col_ref[slot], -1))
        for c in range(column_blocks):
            total = near_adj[c]
            for t in range(GROUP):
                total += products[t] * jnp.where(columns[t] == c, 1.0, 0.0).astype(f32)
            near_adj[c] = total
        return carry

    def forward_group(group, carry):
        products, targets = [], []
        for t in range(GROUP):
            slot = group * GROUP + t
            source = drive_all[tile_col_ref[slot]]
            products.append(dot_nt(source, tiles[slot]))
            targets.append(jnp.where(slot < used, tile_row_ref[slot], -1))
        for i in range(row_blocks):
            total = near_fwd[i]
            for t in range(GROUP):
                total += products[t] * jnp.where(targets[t] == i, 1.0, 0.0).astype(f32)
            near_fwd[i] = total
        return carry

    groups = cap // GROUP
    lax.fori_loop(0, groups // 2, adjoint_group, 0)

    for copy in qz_copies:
        copy.wait_recv()
    piece = q_all.at[b, pl.ds(1, rows - 1)]
    plane_q += [send(piece, piece, qp_sem.at[1, o - 1], blk_at(o, core), r) for o in range(1, chips)]
    piece = q_all.at[b]
    sibling_q = [send(piece, piece, qs_sem.at[0], sibling, r)]

    lax.fori_loop(groups // 2, groups, adjoint_group, 0)
    sib_copies[0].wait_recv()
    for copy in plane_copies:
        copy.wait_recv()
    for j in range(rows):
        total = sib_recv[0, j].astype(f32)
        for o in range(chips - 1):
            total += plane_recv[o, j].astype(f32)
        adj_part[j] = total
        adj_send[j] = total.astype(bf16)
    adj_copies = [
        send(adj_send.at[row_at(o)], adj_recv.at[o - 1], adj_sem.at[o - 1], b, row_at(o))
        for o in range(1, rows)
    ]

    for c in range(column_blocks):
        near_send[c] = near_adj[c].astype(bf16)
    near_copies = [
        send(
            near_send.at[pl.ds(row_at(o) * row_blocks, row_blocks)],
            near_recv.at[o - 1],
            near_sem.at[o - 1],
            b,
            row_at(o),
        )
        for o in range(1, rows)
    ]

    for o in range(1, chips):
        plane_q[o - 1].wait_recv()
        plane_q[chips - 2 + o].wait_recv()
        piece = q_all.at[blk_at(-o, core)]
        sibling_q.append(send(piece, piece, qs_sem.at[o], sibling, r))

    for copy in drive_copies:
        copy.wait_recv()
    lax.fori_loop(0, groups // 2, forward_group, 0)

    for copy in adj_copies:
        copy.wait_recv()
    adjoint = adj_part[r]
    for o in range(rows - 1):
        adjoint += adj_recv[o].astype(f32)
    adj_all[r] = adjoint.astype(bf16)
    piece = adj_all.at[r]
    adjall_copies = [send(piece, piece, adjall_sem.at[o - 1], b, row_at(o)) for o in range(1, rows)]

    for copy in sibling_q:
        copy.wait_recv()
    potential = jnp.zeros((excite, share), f32)
    for z in range(rows):
        columns = pl.ds(pl.multiple_of(row_at(-z) * share, share), share)
        for d in range(1, offsets + 1):
            source = q_all[lax.rem(b - d + clusters, clusters), z]
            potential += dot_nt(source, trans_low[d - 1, :, columns])
    pot_all[r] = potential.astype(bf16)
    piece = pot_all.at[r]
    pot_copies = [send(piece, piece, pot_sem.at[o - 1], b, row_at(o)) for o in range(1, rows)]

    lax.fori_loop(groups // 2, groups, forward_group, 0)

    for copy in near_copies:
        copy.wait_recv()
    for i in range(row_blocks):
        total = near_adj[r * row_blocks + i]
        for o in range(rows - 1):
            total += near_recv[o, i].astype(f32)
        near_adj[r * row_blocks + i] = total

    for copy in pot_copies:
        copy.wait_recv()
    for i in range(row_blocks):
        total = near_fwd[i]
        for j in range(rows):
            block = skout[j * share : (j + 1) * share, i * size : (i + 1) * size]
            total += dot_nn(pot_all[j], block)
        response_ref[:, i * size : (i + 1) * size] = total
    put_response = fetch(response_ref, response_hbm)
    for copy in adjall_copies:
        copy.wait_recv()
    for i in range(row_blocks):
        total = near_adj[r * row_blocks + i]
        for j in range(rows):
            block = skin[j * share : (j + 1) * share, i * size : (i + 1) * size]
            total += dot_nn(adj_all[j], block)
        sensitivity_ref[:, i * size : (i + 1) * size] = total
    put_sensitivity = fetch(sensitivity_ref, sensitivity_hbm)
    for copy in sent:
        copy.wait_send()
    put_response.wait()
    put_sensitivity.wait()


def landing(response, sensitivity, response_out, sensitivity_out):
    response_out[...] = response[...]
    sensitivity_out[...] = sensitivity[...]


def fused_plan(
    rows,
    clusters,
    excitations,
    adjoint_loads,
    near_tiles,
    tile_rows,
    tile_cols,
    tile_count,
    skeleton_in,
    skeleton_out,
    translation,
):
    kernels = translation[0]
    excite, panels = excitations.shape
    cap, size = near_tiles.shape[:2]
    offsets, share, points = kernels.shape
    chips = clusters // 2
    row_blocks = panels // size
    blocks = rows * row_blocks
    others = rows - 1
    sends = 7 * others + 4 * chips - 2 + chips - 1 + others
    vmem, dma = pltpu.VMEM, pltpu.SemaphoreType.DMA
    scratch = [
        vmem((excite, panels), f32),
        vmem((excite, panels), f32),
        pltpu.SMEM(tile_rows.shape, jnp.int32),
        pltpu.SMEM(tile_cols.shape, jnp.int32),
        vmem((excite, panels), f32),
        vmem((excite, panels), f32),
        vmem((cap, size, size), bf16),
        vmem((points, panels), bf16),
        vmem((points, panels), bf16),
        vmem((offsets, share, points), f32),
        vmem((offsets, share, points), bf16),
        vmem((blocks, excite, size), bf16),
        vmem((row_blocks, excite, size), bf16),
        vmem((rows, excite, share), f32),
        vmem((rows, excite, share), bf16),
        vmem((others, excite, share), bf16),
        vmem((rows, excite, share), f32),
        vmem((rows, excite, share), bf16),
        vmem((others, excite, share), bf16),
        vmem((clusters, rows, excite, share), bf16),
        vmem((chips, rows, excite, share), bf16),
        vmem((chips, rows, excite, share), bf16),
        vmem((chips - 1, rows, excite, share), bf16),
        vmem((chips - 1, rows, excite, share), bf16),
        vmem((rows, excite, share), f32),
        vmem((rows, excite, share), bf16),
        vmem((others, excite, share), bf16),
        vmem((rows, excite, share), bf16),
        vmem((rows, excite, share), bf16),
        vmem((row_blocks, excite, size), f32),
        vmem((blocks, excite, size), f32),
        vmem((blocks, excite, size), bf16),
        vmem((others, row_blocks, excite, size), bf16),
        dma((offsets + 9,)),
        dma((sends,)),
        dma((others,)),
        dma((others,)),
        dma((others,)),
        dma((others,)),
        dma((2, chips - 1)),
        dma((chips,)),
        dma((chips,)),
        dma((chips - 1,)),
        dma((others,)),
        dma((others,)),
        dma((others,)),
        dma((others,)),
    ]
    whole_vmem = pl.BlockSpec(memory_space=pltpu.VMEM)
    anywhere = pl.BlockSpec(memory_space=pl.ANY)
    results = pl.pallas_call(
        functools.partial(kernel, rows, clusters),
        out_shape=[jax.ShapeDtypeStruct((excite, panels), f32)] * 2,
        in_specs=[pl.BlockSpec(memory_space=pltpu.SMEM)] + [anywhere] * 8,
        out_specs=[anywhere] * 2,
        scratch_shapes=scratch,
        compiler_params=pltpu.CompilerParams(
            collective_id=0, has_side_effects=True, vmem_limit_bytes=VMEM_BYTES
        ),
    )(
        tile_count,
        tile_rows,
        tile_cols,
        excitations,
        adjoint_loads,
        near_tiles,
        skeleton_in,
        skeleton_out,
        kernels,
    )
    return pl.pallas_call(
        landing,
        out_shape=[jax.ShapeDtypeStruct((excite, panels), f32)] * 2,
        in_specs=[whole_vmem] * 2,
        out_specs=[whole_vmem] * 2,
        compiler_params=pltpu.CompilerParams(vmem_limit_bytes=VMEM_BYTES),
    )(*results)


def solution(mesh):
    clusters, rows = mesh.shape["blk"], mesh.shape["rows"]

    def on_device(*args):
        share = args[8].shape[2]
        tile_size = args[2].shape[1]
        fits = clusters == 8 and rows == 4 and share % 128 == 0
        if fits and tile_size % 128 == 0 and args[2].shape[0] % (2 * GROUP) == 0:
            return tuple(fused_plan(rows, clusters, *args))
        return plain_plan(*args)

    return jax.shard_map(
        on_device,
        mesh=mesh,
        in_specs=(
            P(None, ("blk", "rows")),
            P(None, ("blk", "rows")),
            P(("blk", "rows"), None, None),
            P(("blk", "rows")),
            P(("blk", "rows")),
            P(("blk", "rows")),
            P(None, ("blk", "rows")),
            P(None, ("blk", "rows")),
            P("blk", None, "rows", None),
        ),
        out_specs=(P(None, ("blk", "rows")), P(None, ("blk", "rows"))),
        check_vma=False,
    )
```

```python
import functools

import jax
import jax.numpy as jnp
from jax import lax
from jax.experimental import pallas as pl
from jax.experimental.pallas import tpu as pltpu
from jax.sharding import PartitionSpec as P

highest = lax.Precision.HIGHEST


def plain_plan(
    excitations,
    adjoint_loads,
    near_tiles,
    tile_rows,
    tile_cols,
    tile_count,
    skeleton_in,
    skeleton_out,
    translation,
):
    drive_low = excitations.astype(jnp.bfloat16)
    loads_low = adjoint_loads.astype(jnp.bfloat16)
    excite_count = excitations.shape[0]
    panels = excitations.shape[1]
    tile_size = near_tiles.shape[1]
    kernels = translation[0]
    share_width = kernels.shape[1]
    clusters = lax.axis_size("blk")
    cluster = lax.axis_index("blk")
    gathered = lax.all_gather(drive_low, "rows", axis=1, tiled=True)
    column_blocks = gathered.shape[1] // tile_size
    row_blocks = panels // tile_size
    drive_blocks = gathered.reshape(excite_count, column_blocks, tile_size)
    load_blocks = loads_low.reshape(excite_count, row_blocks, tile_size)
    used_slots = tile_count[0]

    def near_group(group_index, carry):
        ahead, behind = carry
        first_slot = group_index * 4
        tile_group = lax.dynamic_slice_in_dim(near_tiles, first_slot, 4, 0)
        row_ids = lax.dynamic_slice_in_dim(tile_rows, first_slot, 4, 0)
        column_ids = lax.dynamic_slice_in_dim(tile_cols, first_slot, 4, 0)
        live_mask = (first_slot + jnp.arange(4, dtype=jnp.int32) < used_slots).astype(jnp.float32)[
            None, :, None
        ]
        source = jnp.take(drive_blocks, column_ids, axis=1)
        target = jnp.take(load_blocks, row_ids, axis=1)
        forward = (
            jnp.einsum("egj,gij->egi", source, tile_group, preferred_element_type=jnp.float32)
            * live_mask
        )
        backward = (
            jnp.einsum("egi,gij->egj", target, tile_group, preferred_element_type=jnp.float32)
            * live_mask
        )
        return (ahead.at[:, row_ids].add(forward), behind.at[:, column_ids].add(backward))

    near_start = (
        jnp.zeros((excite_count, row_blocks, tile_size), jnp.float32),
        jnp.zeros((excite_count, column_blocks, tile_size), jnp.float32),
    )
    near_ahead, near_behind = lax.fori_loop(0, (used_slots + 3) // 4, near_group, near_start)
    contract_panels = (((1,), (1,)), ((), ()))
    charge_part = lax.dot_general(
        drive_low, skeleton_in, contract_panels, preferred_element_type=jnp.float32
    )
    gradient_part = lax.dot_general(
        loads_low, skeleton_out, contract_panels, preferred_element_type=jnp.float32
    )
    charges, gradient_all = lax.psum((charge_part, gradient_part), "rows")
    gradient = lax.dynamic_slice_in_dim(
        gradient_all, lax.axis_index("rows") * share_width, share_width, 1
    )

    def offsets_for(other_ids):
        offset = jnp.remainder(cluster - other_ids, clusters)
        active = (offset != 0).astype(jnp.float32)
        return (jnp.maximum(offset - 1, 0), active)

    charge_piece = lax.all_gather(charges[None], "blk", axis=0, tiled=True)
    span_count = charge_piece.shape[0]
    offset, active = offsets_for(jnp.arange(span_count, dtype=jnp.int32))
    chosen = jnp.take(kernels, offset, axis=0)
    potential = jnp.einsum(
        "cej,ckj->ek", charge_piece * active[:, None, None], chosen, precision=highest
    )
    potential_low = lax.all_gather(potential.astype(jnp.bfloat16), "rows", axis=1, tiled=True)
    far_ahead = jnp.dot(potential_low, skeleton_out, preferred_element_type=jnp.float32)
    offset, active = offsets_for(jnp.arange(lax.axis_size("blk") * 1, dtype=jnp.int32))
    chosen = jnp.take(kernels, offset, axis=0)
    summed = lax.psum_scatter(
        jnp.einsum("ek,ckj->cej", gradient, chosen, precision=highest) * active[:, None, None],
        "blk",
        scatter_dimension=0,
        tiled=True,
    )
    adjoint_low = lax.psum(summed[0], "rows").astype(jnp.bfloat16)
    far_behind = jnp.dot(adjoint_low, skeleton_in, preferred_element_type=jnp.float32)
    near_columns = lax.psum_scatter(
        near_behind.reshape(excite_count, column_blocks * tile_size),
        "rows",
        scatter_dimension=1,
        tiled=True,
    )
    response = near_ahead.reshape(excite_count, panels) + far_ahead
    sensitivity = near_columns + far_behind
    return (response, sensitivity)


MESH = pl.DeviceIdType.MESH
GROUP = 4
VMEM_BYTES = 62 * 1024 * 1024
bf16 = jnp.bfloat16
f32 = jnp.float32


def dot_nt(a, b):
    return lax.dot_general(a, b, (((1,), (1,)), ((), ())), preferred_element_type=f32)


def dot_nn(a, b):
    return jnp.dot(a, b, preferred_element_type=f32)


def kernel(
    rows,
    clusters,
    count_ref,
    tile_row_hbm,
    tile_col_hbm,
    drive_hbm,
    loads_hbm,
    tiles_hbm,
    skin_hbm,
    skout_hbm,
    trans_hbm,
    response_hbm,
    sensitivity_hbm,
    response_ref,
    sensitivity_ref,
    tile_row_ref,
    tile_col_ref,
    drive_ref,
    loads_ref,
    tiles,
    skin,
    skout,
    trans,
    trans_low,
    drive_all,
    loads_low,
    grad_part,
    grad_send,
    grad_recv,
    charge_part,
    charge_send,
    charge_recv,
    q_all,
    sib_send,
    sib_recv,
    plane_send,
    plane_recv,
    adj_part,
    adj_send,
    adj_recv,
    adj_all,
    pot_all,
    near_fwd,
    near_adj,
    near_send,
    near_recv,
    local_sem,
    send_sem,
    grad_sem,
    charge_sem,
    drive_sem,
    qz_sem,
    qp_sem,
    qs_sem,
    sib_sem,
    plane_sem,
    adj_sem,
    adjall_sem,
    pot_sem,
    near_sem,
):
    chips = clusters // 2
    b = lax.axis_index("blk")
    r = lax.axis_index("rows")
    core = lax.rem(b, 2)
    chip = lax.div(b, 2)
    cap, size = tiles.shape[0], tiles.shape[1]
    share = q_all.shape[3]
    row_blocks = loads_low.shape[0]
    column_blocks = rows * row_blocks
    offsets = trans.shape[0]

    def row_at(step):
        return lax.rem(r + step + rows, rows)

    def blk_at(step, which):
        return lax.rem(chip + step + chips, chips) * 2 + which

    sibling = b + 1 - 2 * core

    local = []

    def fetch(src, dst):
        copy = pltpu.make_async_copy(src, dst, local_sem.at[len(local)])
        copy.start()
        local.append(copy)
        return copy

    get_loads = fetch(loads_hbm, loads_ref)
    get_out = fetch(skout_hbm, skout)
    get_drive = fetch(drive_hbm, drive_ref)
    get_in = fetch(skin_hbm, skin)
    sent = []

    def send(src, dst, recv, blk, row):
        copy = pltpu.make_async_remote_copy(
            src_ref=src,
            dst_ref=dst,
            send_sem=send_sem.at[len(sent)],
            recv_sem=recv,
            device_id=(blk, row),
            device_id_type=MESH,
        )
        copy.start()
        sent.append(copy)
        return copy

    barrier = pltpu.get_barrier_semaphore()
    partners = [(b, row_at(o)) for o in range(1, rows)]
    partners += [(blk_at(o, core), r) for o in range(1, chips)]
    partners += [(sibling, r)]
    for partner in partners:
        pl.semaphore_signal(barrier, inc=1, device_id=partner, device_id_type=MESH)

    get_loads.wait()
    for i in range(row_blocks):
        loads_low[i] = loads_ref[:, i * size : (i + 1) * size].astype(bf16)
    loads_wide = loads_ref[...].astype(bf16)
    get_out.wait()
    get_trans = [fetch(trans_hbm.at[d], trans.at[d]) for d in range(offsets)]
    get_lists = [
        fetch(tile_row_hbm, tile_row_ref),
        fetch(tile_col_hbm, tile_col_ref),
    ]
    for j in range(rows):
        part = dot_nt(loads_wide, skout[j * share : (j + 1) * share, :])
        grad_part[j] = part
        grad_send[j] = part.astype(bf16)
    pl.semaphore_wait(barrier, len(partners))
    grad_copies = [
        send(grad_send.at[row_at(o)], grad_recv.at[o - 1], grad_sem.at[o - 1], b, row_at(o))
        for o in range(1, rows)
    ]
    get_drive.wait()
    for i in range(row_blocks):
        drive_all[r * row_blocks + i] = drive_ref[:, i * size : (i + 1) * size].astype(bf16)
    drive_wide = drive_ref[...].astype(bf16)
    get_in.wait()
    get_tiles = fetch(tiles_hbm, tiles)
    for j in range(rows):
        part = dot_nt(drive_wide, skin[j * share : (j + 1) * share, :])
        charge_part[j] = part
        charge_send[j] = part.astype(bf16)
    charge_copies = [
        send(charge_send.at[row_at(o)], charge_recv.at[o - 1], charge_sem.at[o - 1], b, row_at(o))
        for o in range(1, rows)
    ]

    for d in range(offsets):
        get_trans[d].wait()
        trans_low[d] = trans[d].astype(bf16)

    for copy in grad_copies:
        copy.wait_recv()
    gradient = grad_part[r]
    for o in range(rows - 1):
        gradient += grad_recv[o].astype(f32)
    grad_high = gradient.astype(bf16)
    grad_rest = (gradient - grad_high.astype(f32)).astype(bf16)
    grad_both = jnp.concatenate([grad_high, grad_rest], axis=0)
    excite = gradient.shape[0]

    def adjoint_term(target, j):
        index = lax.rem(b - target + clusters, clusters) - 1
        both = dot_nn(grad_both, trans_low[index, :, j * share : (j + 1) * share])
        return both[:excite] + both[excite:]

    sib_copies = [None] * chips
    for o in [*range(1, chips), 0]:
        for j in range(rows):
            sib_send[o, j] = adjoint_term(blk_at(o, 1 - core), j).astype(bf16)
        sib_copies[o] = send(sib_send.at[o], sib_recv.at[o], sib_sem.at[o], sibling, r)

    for copy in charge_copies:
        copy.wait_recv()
    charge = charge_part[r]
    for o in range(rows - 1):
        charge += charge_recv[o].astype(f32)
    q_all[b, 0] = charge.astype(bf16)
    piece = q_all.at[b, 0]
    qz_copies = [
        send(piece, q_all.at[b, o], qz_sem.at[o - 1], b, row_at(o)) for o in range(1, rows)
    ]
    plane_q = [send(piece, piece, qp_sem.at[0, o - 1], blk_at(o, core), r) for o in range(1, chips)]

    mine = pl.ds(r * row_blocks, row_blocks)
    drive_copies = [
        send(drive_all.at[mine], drive_all.at[mine], drive_sem.at[o - 1], b, row_at(o))
        for o in range(1, rows)
    ]

    plane_copies = []
    for o in range(1, chips):
        terms = [adjoint_term(blk_at(o, core), j) for j in range(rows)]
        sib_copies[o].wait_recv()
        for j in range(rows):
            plane_send[o - 1, j] = (terms[j] + sib_recv[o, j].astype(f32)).astype(bf16)
        plane_copies.append(
            send(
                plane_send.at[o - 1],
                plane_recv.at[o - 1],
                plane_sem.at[o - 1],
                blk_at(o, core),
                r,
            )
        )

    near_adj[...] = jnp.zeros_like(near_adj)
    near_fwd[...] = jnp.zeros_like(near_fwd)
    get_tiles.wait()
    for copy in get_lists:
        copy.wait()

    used = count_ref[0]

    def adjoint_group(group, carry):
        products, columns = [], []
        for t in range(GROUP):
            slot = group * GROUP + t
            source = loads_low[tile_row_ref[slot]]
            products.append(dot_nn(source, tiles[slot]))
            columns.append(jnp.where(slot < used, tile_col_ref[slot], -1))
        for c in range(column_blocks):
            total = near_adj[c]
            for t in range(GROUP):
                total += products[t] * jnp.where(columns[t] == c, 1.0, 0.0).astype(f32)
            near_adj[c] = total
        return carry

    def forward_group(group, carry):
        products, targets = [], []
        for t in range(GROUP):
            slot = group * GROUP + t
            source = drive_all[tile_col_ref[slot]]
            products.append(dot_nt(source, tiles[slot]))
            targets.append(jnp.where(slot < used, tile_row_ref[slot], -1))
        for i in range(row_blocks):
            total = near_fwd[i]
            for t in range(GROUP):
                total += products[t] * jnp.where(targets[t] == i, 1.0, 0.0).astype(f32)
            near_fwd[i] = total
        return carry

    groups = cap // GROUP
    lax.fori_loop(0, groups // 2, adjoint_group, 0)

    for copy in qz_copies:
        copy.wait_recv()
    piece = q_all.at[b, pl.ds(1, rows - 1)]
    plane_q += [send(piece, piece, qp_sem.at[1, o - 1], blk_at(o, core), r) for o in range(1, chips)]
    piece = q_all.at[b]
    sibling_q = [send(piece, piece, qs_sem.at[0], sibling, r)]

    sib_copies[0].wait_recv()
    for copy in plane_copies:
        copy.wait_recv()
    for j in range(rows):
        total = sib_recv[0, j].astype(f32)
        for o in range(chips - 1):
            total += plane_recv[o, j].astype(f32)
        adj_part[j] = total
        adj_send[j] = total.astype(bf16)
    adj_copies = [
        send(adj_send.at[row_at(o)], adj_recv.at[o - 1], adj_sem.at[o - 1], b, row_at(o))
        for o in range(1, rows)
    ]

    for o in range(1, chips):
        plane_q[o - 1].wait_recv()
        plane_q[chips - 2 + o].wait_recv()
        piece = q_all.at[blk_at(-o, core)]
        sibling_q.append(send(piece, piece, qs_sem.at[o], sibling, r))

    lax.fori_loop(groups // 2, groups, adjoint_group, 0)
    for c in range(column_blocks):
        near_send[c] = near_adj[c].astype(bf16)
    near_copies = [
        send(
            near_send.at[pl.ds(row_at(o) * row_blocks, row_blocks)],
            near_recv.at[o - 1],
            near_sem.at[o - 1],
            b,
            row_at(o),
        )
        for o in range(1, rows)
    ]

    for copy in drive_copies:
        copy.wait_recv()
    lax.fori_loop(0, groups // 4, forward_group, 0)

    for copy in adj_copies:
        copy.wait_recv()
    adjoint = adj_part[r]
    for o in range(rows - 1):
        adjoint += adj_recv[o].astype(f32)
    adj_all[r] = adjoint.astype(bf16)
    piece = adj_all.at[r]
    adjall_copies = [send(piece, piece, adjall_sem.at[o - 1], b, row_at(o)) for o in range(1, rows)]

    for copy in sibling_q:
        copy.wait_recv()
    potential = jnp.zeros((excite, share), f32)
    for z in range(rows):
        columns = pl.ds(pl.multiple_of(row_at(-z) * share, share), share)
        for d in range(1, offsets + 1):
            source = q_all[lax.rem(b - d + clusters, clusters), z]
            potential += dot_nt(source, trans_low[d - 1, :, columns])
    pot_all[r] = potential.astype(bf16)
    piece = pot_all.at[r]
    pot_copies = [send(piece, piece, pot_sem.at[o - 1], b, row_at(o)) for o in range(1, rows)]

    lax.fori_loop(groups // 4, groups, forward_group, 0)

    for copy in near_copies:
        copy.wait_recv()
    for i in range(row_blocks):
        total = near_adj[r * row_blocks + i]
        for o in range(rows - 1):
            total += near_recv[o, i].astype(f32)
        near_adj[r * row_blocks + i] = total

    for copy in pot_copies:
        copy.wait_recv()
    for i in range(row_blocks):
        total = near_fwd[i]
        for j in range(rows):
            block = skout[j * share : (j + 1) * share, i * size : (i + 1) * size]
            total += dot_nn(pot_all[j], block)
        response_ref[:, i * size : (i + 1) * size] = total
    put_response = fetch(response_ref, response_hbm)
    for copy in adjall_copies:
        copy.wait_recv()
    for i in range(row_blocks):
        total = near_adj[r * row_blocks + i]
        for j in range(rows):
            block = skin[j * share : (j + 1) * share, i * size : (i + 1) * size]
            total += dot_nn(adj_all[j], block)
        sensitivity_ref[:, i * size : (i + 1) * size] = total
    put_sensitivity = fetch(sensitivity_ref, sensitivity_hbm)
    for copy in sent:
        copy.wait_send()
    put_response.wait()
    put_sensitivity.wait()


def landing(response, sensitivity, response_out, sensitivity_out):
    response_out[...] = response[...]
    sensitivity_out[...] = sensitivity[...]


def fused_plan(
    rows,
    clusters,
    excitations,
    adjoint_loads,
    near_tiles,
    tile_rows,
    tile_cols,
    tile_count,
    skeleton_in,
    skeleton_out,
    translation,
):
    kernels = translation[0]
    excite, panels = excitations.shape
    cap, size = near_tiles.shape[:2]
    offsets, share, points = kernels.shape
    chips = clusters // 2
    row_blocks = panels // size
    blocks = rows * row_blocks
    others = rows - 1
    sends = 7 * others + 4 * chips - 2 + chips - 1 + others
    vmem, dma = pltpu.VMEM, pltpu.SemaphoreType.DMA
    scratch = [
        vmem((excite, panels), f32),
        vmem((excite, panels), f32),
        pltpu.SMEM(tile_rows.shape, jnp.int32),
        pltpu.SMEM(tile_cols.shape, jnp.int32),
        vmem((excite, panels), f32),
        vmem((excite, panels), f32),
        vmem((cap, size, size), bf16),
        vmem((points, panels), bf16),
        vmem((points, panels), bf16),
        vmem((offsets, share, points), f32),
        vmem((offsets, share, points), bf16),
        vmem((blocks, excite, size), bf16),
        vmem((row_blocks, excite, size), bf16),
        vmem((rows, excite, share), f32),
        vmem((rows, excite, share), bf16),
        vmem((others, excite, share), bf16),
        vmem((rows, excite, share), f32),
        vmem((rows, excite, share), bf16),
        vmem((others, excite, share), bf16),
        vmem((clusters, rows, excite, share), bf16),
        vmem((chips, rows, excite, share), bf16),
        vmem((chips, rows, excite, share), bf16),
        vmem((chips - 1, rows, excite, share), bf16),
        vmem((chips - 1, rows, excite, share), bf16),
        vmem((rows, excite, share), f32),
        vmem((rows, excite, share), bf16),
        vmem((others, excite, share), bf16),
        vmem((rows, excite, share), bf16),
        vmem((rows, excite, share), bf16),
        vmem((row_blocks, excite, size), f32),
        vmem((blocks, excite, size), f32),
        vmem((blocks, excite, size), bf16),
        vmem((others, row_blocks, excite, size), bf16),
        dma((offsets + 9,)),
        dma((sends,)),
        dma((others,)),
        dma((others,)),
        dma((others,)),
        dma((others,)),
        dma((2, chips - 1)),
        dma((chips,)),
        dma((chips,)),
        dma((chips - 1,)),
        dma((others,)),
        dma((others,)),
        dma((others,)),
        dma((others,)),
    ]
    whole_vmem = pl.BlockSpec(memory_space=pltpu.VMEM)
    anywhere = pl.BlockSpec(memory_space=pl.ANY)
    results = pl.pallas_call(
        functools.partial(kernel, rows, clusters),
        out_shape=[jax.ShapeDtypeStruct((excite, panels), f32)] * 2,
        in_specs=[pl.BlockSpec(memory_space=pltpu.SMEM)] + [anywhere] * 8,
        out_specs=[anywhere] * 2,
        scratch_shapes=scratch,
        compiler_params=pltpu.CompilerParams(
            collective_id=0, has_side_effects=True, vmem_limit_bytes=VMEM_BYTES
        ),
    )(
        tile_count,
        tile_rows,
        tile_cols,
        excitations,
        adjoint_loads,
        near_tiles,
        skeleton_in,
        skeleton_out,
        kernels,
    )
    return pl.pallas_call(
        landing,
        out_shape=[jax.ShapeDtypeStruct((excite, panels), f32)] * 2,
        in_specs=[whole_vmem] * 2,
        out_specs=[whole_vmem] * 2,
        compiler_params=pltpu.CompilerParams(vmem_limit_bytes=VMEM_BYTES),
    )(*results)


def solution(mesh):
    clusters, rows = mesh.shape["blk"], mesh.shape["rows"]

    def on_device(*args):
        share = args[8].shape[2]
        tile_size = args[2].shape[1]
        fits = clusters == 8 and rows == 4 and share % 128 == 0
        if fits and tile_size % 128 == 0 and args[2].shape[0] % (2 * GROUP) == 0:
            return tuple(fused_plan(rows, clusters, *args))
        return plain_plan(*args)

    return jax.shard_map(
        on_device,
        mesh=mesh,
        in_specs=(
            P(None, ("blk", "rows")),
            P(None, ("blk", "rows")),
            P(("blk", "rows"), None, None),
            P(("blk", "rows")),
            P(("blk", "rows")),
            P(("blk", "rows")),
            P(None, ("blk", "rows")),
            P(None, ("blk", "rows")),
            P("blk", None, "rows", None),
        ),
        out_specs=(P(None, ("blk", "rows")), P(None, ("blk", "rows"))),
        check_vma=False,
    )
```
